32 devices in a mesh: dp: 2 (over core), seq: 4 (over y, x), tensor: 4 (over z).
Axes of the slice: x: 2, y: 2, z: 4, core: 2. Of those that a mesh axis runs over, the one named last changes fastest.
Arguments:
- hidden: bfloat16 [4096, 7168], P(('dp', 'seq')), may hold values from -34 to 34
- grad_out: bfloat16 [4096, 4096], P(('dp', 'seq'), 'tensor'), may hold values from -24 to 24
- master_weight: float32 [7168, 4096], P(('dp', 'seq'), 'tensor'), may hold values from -6 to 6
- row_prev: float32 [7168], P(('dp', 'seq')), may hold values from 0.01 to 0.3
- col_prev: float32 [4096], P('tensor'), may hold values from 0.01 to 0.3
Outputs:
- new_weight: bfloat16 [7168, 4096], P('dp', 'tensor')
- update: float32 [7168, 4096], P(('dp', 'seq'), 'tensor')
- new_rows: float32 [7168], P(('dp', 'seq'))
- new_cols: float32 [4096], P('tensor')
The draws below stay inside these ranges and needn't reach their ends.
All inputs are finite; a program needn't handle non-finite values.
Results may differ from the reference program's by a relative error of at most 0.0004.
Values may be sent and summed in bfloat16 or wider, within the bound.
No kernel may reach another device: no remote copies, remote signals or barrier semaphores. Data moves between devices by JAX's collectives and lax.ppermute only.
A program may use at most 128 MiB of HBM per device.

```python
import math
import jax
import jax.numpy as jnp
from jax import lax

D = 4096
FF_WIN = 7168
TOKENS = 4096


def hidden_parts(key):
    first, second = jax.random.split(jax.random.fold_in(key, 11), 2)
    ramp = jnp.arange(FF_WIN).astype(jnp.float32) / FF_WIN - 0.5
    unit = jnp.exp(jax.random.uniform(first, (FF_WIN,), minval=-1.15, maxval=1.15)) * jnp.exp(math.log(3.0) * ramp)
    values = jax.random.truncated_normal(second, -4.0, 4.0, (TOKENS, FF_WIN)) * unit
    return (values, unit)


def draw_hidden(key, part):
    values, unit = hidden_parts(key)
    return values.astype(jnp.bfloat16)


def draw_grad_out(key, part):
    values, unit = hidden_parts(key)
    first, second, third = jax.random.split(jax.random.fold_in(key, 23), 3)
    ramp = jnp.arange(D).astype(jnp.float32) / D - 0.5
    column = jnp.exp(jax.random.uniform(first, (D,), minval=-1.15, maxval=1.15)) * jnp.exp(math.log(3.0) * ramp)
    column = column / jnp.sqrt(jnp.float32(TOKENS))
    chosen = jax.random.permutation(third, FF_WIN)[:D]
    carried = values[:, chosen] / unit[chosen][None, :]
    strength = 0.4 * jnp.sqrt(jnp.float32(D) / jnp.float32(TOKENS))
    noise = jax.random.truncated_normal(second, -4.0, 4.0, (TOKENS, D))
    values_out = (0.5 * noise + strength * carried) * column[None, :]
    return values_out.astype(jnp.bfloat16)


def steps_of(key, extent, cuts, least, largest):
    def one(position, blocks):
        heights = jax.random.uniform(jax.random.fold_in(jax.random.fold_in(key, 6), position), (blocks,), jnp.float32, least / len(cuts), largest / len(cuts))
        return jnp.repeat(jnp.exp(heights), extent[position] // blocks).reshape((-1,) + (1,) * (len(extent) - position - 1))

    loudness = one(*cuts[0])
    for cut in cuts[1:]:
        loudness = loudness * one(*cut)
    return loudness


def gaussian(key, dims, spread, bound, shards=(), dtype=jnp.bfloat16):
    result = spread * jax.random.normal(key, dims, jnp.float32)
    if shards:
        result = result * steps_of(key, dims, shards, -0.22, 0.18)
    return jnp.clip(result, -bound, bound).astype(dtype)


def setup_inputs(seed: int = 0) -> dict:
    seeds = jax.random.split(jax.random.key(seed), 6)
    hidden = draw_hidden(jax.random.fold_in(seeds[5], 71), 0)
    grad_out = draw_grad_out(jax.random.fold_in(seeds[5], 71), 0)
    master_weight = gaussian(seeds[2], (FF_WIN, D), 1.0, 6.0, ((0, 8), (1, 4)), jnp.float32)
    row_prev = jnp.clip(jnp.exp(math.log(0.3) - 3.4011974 * jax.random.uniform(seeds[3], (FF_WIN,), jnp.float32) ** steps_of(seeds[3], (FF_WIN,), ((0, 8),), -0.2, 0.2)), 0.01, 0.3)
    col_prev = jnp.clip(jnp.exp(math.log(0.3) - 3.4011974 * jax.random.uniform(seeds[4], (D,), jnp.float32) ** steps_of(seeds[4], (D,), ((0, 4),), -0.2, 0.2)), 0.01, 0.3)
    return dict(hidden=hidden, grad_out=grad_out, master_weight=master_weight, row_prev=row_prev, col_prev=col_prev)


decay_rate = 0.8
learn_rate = 0.05
small_term = 1e-06

def reference(hidden, grad_out, master_weight, row_prev, col_prev):
    grads = lax.dot_general(hidden, grad_out, (((0,), (0,)), ((), ())), preferred_element_type=jnp.float32)
    squares = grads * grads + small_term
    new_rows = decay_rate * row_prev + (1.0 - decay_rate) * lax.optimization_barrier(jnp.sum(squares, axis=1)) / D
    new_cols = decay_rate * col_prev + (1.0 - decay_rate) * lax.optimization_barrier(jnp.sum(squares, axis=0)) / FF_WIN
    second = new_rows[:, None] * new_cols[None, :]
    raw = grads / jnp.sqrt(second)
    size = jnp.sqrt(jnp.sum(raw * raw) / (FF_WIN * D))
    update = raw / jnp.maximum(1.0, size)
    new_weight = (master_weight - learn_rate * update).astype(jnp.bfloat16)
    return (new_weight, update, new_rows, new_cols)
```

```python
import functools
import math

import jax
import jax.numpy as jnp
import numpy as np
from jax import lax
from jax.experimental import pallas as pl
from jax.experimental.pallas import tpu as pltpu
from jax.sharding import PartitionSpec as P

decay_rate = 0.8
learn_rate = 0.05
small_term = 1e-06

POWER = 11
TOP = 2.0 ** (125.0 / POWER)
TAIL = 16
VMEM_LIMIT = 16 * 2**20


def chunk_of(rows):
    return 128 if rows % 128 == 0 else rows


def encode(x):
    top = jnp.max(jnp.abs(x), axis=0, keepdims=True)
    scale = jnp.maximum(top * 1.004, 1e-30).astype(jnp.bfloat16).astype(jnp.float32)
    u = x * (TOP / scale)
    u2 = u * u
    u4 = u2 * u2
    return (u4 * u4 * u2 * u).astype(jnp.bfloat16), scale


def decode(code, scale):
    code = code.astype(jnp.float32)
    size = jnp.abs(code)
    u = jnp.exp(jnp.log(jnp.maximum(size, 1e-37)) * (1.0 / POWER)) * (scale * (1.0 / TOP))
    return jnp.where(size > 1e-37, jnp.where(code > 0, u, -u), 0.0)


def write_scales(ref, scales):
    rows, cols = ref.shape
    at = lax.broadcasted_iota(jnp.int32, (TAIL, cols), 0)
    tail = jnp.zeros((TAIL, cols), jnp.float32)
    for j, scale in enumerate(scales):
        tail = jnp.where(at == j, scale, tail)
    ref[rows - TAIL :] = tail.astype(jnp.bfloat16)


def read_scales(ref):
    return ref[ref.shape[0] - TAIL :].astype(jnp.float32)


def pieces_of(rows):
    n = rows // 128
    cuts = sorted({0, (n + 2) // 4, (n + 1) // 2, n})
    return [slice(a * 128, b * 128) for a, b in zip(cuts, cuts[1:])]


def product_kernel(layout, entry, coded, *refs):
    copied, n_hs, n_base = layout
    refs = list(refs)
    take = lambda k: [refs.pop(0) for _ in range(k)]
    source, hs = take(2 * copied), take(n_hs)
    gs, bases, outs = take(n_hs + copied), take(n_base), take(2)
    arriving = {}
    if copied:
        (table, hidden), (held, sems) = source, refs
        start = pl.multiple_of(table[entry], 128)
        for k, at in enumerate(pieces_of(held.shape[1])):
            there = pl.ds(pl.multiple_of(start + at.start, 128), at.stop - at.start)
            copy = pltpu.make_async_copy(hidden.at[:, there], held.at[:, at], sems.at[k])
            copy.start()
            arriving[at.start] = copy
        hs = [held] + hs
    rows, cols = hs[0].shape[1], gs[0].shape[1]
    half, chunk = cols // 2, chunk_of(rows)
    scales = [[], []]
    for j in range(rows // chunk):
        at = slice(j * chunk, (j + 1) * chunk)
        if at.start in arriving:
            arriving[at.start].wait()
        total = None
        for h, g in zip(hs, gs):
            term = lax.dot_general(
                h[:, at], g[...], (((0,), (0,)), ((), ())), preferred_element_type=jnp.float32
            )
            total = term if total is None else total + term
        for part in (0, 1):
            x = total[:, part * half : (part + 1) * half]
            if bases:
                x = x + bases[part][at]
            if coded[part]:
                outs[part][at], scale = encode(x)
                scales[part].append(scale)
            else:
                outs[part][at] = x
    for part in (0, 1):
        if coded[part]:
            write_scales(outs[part], scales[part])


def slice_kernel(entries, table, hidden, *refs):
    outs, sems = refs[: len(entries)], refs[len(entries)]
    copies = []
    for k, out in enumerate(outs):
        at = pl.ds(pl.multiple_of(table[entries[k]], 128), out.shape[1])
        copies.append(pltpu.make_async_copy(hidden.at[:, at], out, sems.at[k]))
    for copy in copies:
        copy.start()
    for copy in copies:
        copy.wait()


def relay_kernel(n, base, *refs):
    messages, out = refs[:n], refs[n]
    rows = base.shape[0]
    chunk = chunk_of(rows)
    tails = [read_scales(m) for m in messages]
    scales = []
    for j in range(rows // chunk):
        at = slice(j * chunk, (j + 1) * chunk)
        total = base[at]
        for m, tail in zip(messages, tails):
            total = total + decode(m[at], tail[j : j + 1])
        out[at], scale = encode(total)
        scales.append(scale)
    write_scales(out, scales)


def gather_kernel(n, base, *refs):
    messages, out = refs[:n], refs[n]
    rows = base.shape[0]
    chunk = chunk_of(rows)
    tails = [read_scales(m) for m in messages]
    for j in range(rows // chunk):
        at = slice(j * chunk, (j + 1) * chunk)
        total = base[at]
        for m, tail in zip(messages, tails):
            total = total + decode(m[at], tail[j : j + 1])
        out[at] = total


def final_kernel(counts, *refs):
    bases, refs = refs[:2], refs[2:]
    messages = refs[: counts[0]], refs[counts[0] : sum(counts)]
    out, row_out, col_out = refs[sum(counts) :]
    rows, half = bases[0].shape
    chunk = chunk_of(rows)
    tails = [[read_scales(m) for m in group] for group in messages]
    col_sums = [jnp.zeros((1, half), jnp.float32)] * 2
    for j in range(rows // chunk):
        at = slice(j * chunk, (j + 1) * chunk)
        row_sum = jnp.zeros((chunk, 128), jnp.float32)
        for part in (0, 1):
            total = bases[part][at]
            for m, tail in zip(messages[part], tails[part]):
                total = total + decode(m[at], tail[j : j + 1])
            out[at, part * half : (part + 1) * half] = total
            squares = total * total
            col_sums[part] = col_sums[part] + jnp.sum(squares, axis=0, keepdims=True)
            for k in range(half // 128):
                row_sum = row_sum + squares[:, k * 128 : (k + 1) * 128]
        row_out[j : j + 1] = jnp.sum(row_sum.T, axis=0, keepdims=True)
    for part in (0, 1):
        col_out[:, part * half : (part + 1) * half] = col_sums[part]


def as_column(row):
    return jnp.broadcast_to(row, (128, row.shape[1])).T


def rows_kernel(n, all_cols, grads, row_prev, col_part, *refs):
    parts, (rows_out, by_row_out, both_out) = refs[:n], refs[n:]
    total = sum(p[...] for p in parts[1:]) + parts[0][...] if n > 1 else parts[0][...]
    total = total + small_term * all_cols
    new_rows = decay_rate * row_prev[...] + (1.0 - decay_rate) * total / all_cols
    rows_out[...] = new_rows
    by_row_out[...] = 1.0 / jnp.sqrt(new_rows)
    inverse = 1.0 / new_rows
    n_chunks, chunk = new_rows.shape
    cols = grads.shape[1]
    sums = [jnp.zeros((1, 128), jnp.float32)] * (cols // 128)
    for j in range(n_chunks):
        weight = as_column(inverse[j : j + 1])
        for k in range(cols // 128):
            g = grads[j * chunk : (j + 1) * chunk, k * 128 : (k + 1) * 128]
            sums[k] = sums[k] + jnp.sum(g * g * weight, axis=0, keepdims=True)
    both_out[0:1] = col_part[...]
    for k in range(cols // 128):
        both_out[1:2, k * 128 : (k + 1) * 128] = sums[k]


def cols_kernel(n, all_rows, col_prev, *refs):
    parts, (cols_out, by_col_out, total_out) = refs[:n], refs[n:]
    both = sum(p[...] for p in parts[1:]) + parts[0][...] if n > 1 else parts[0][...]
    total = both[0:1] + small_term * all_rows
    new_cols = decay_rate * col_prev[...] + (1.0 - decay_rate) * total / all_rows
    cols_out[...] = new_cols
    by_col_out[...] = 1.0 / jnp.sqrt(new_cols)
    share = jnp.sum(both[1:2] / new_cols, axis=1, keepdims=True)
    total_out[...] = jnp.broadcast_to(share, total_out.shape)


def factors(elements, parts, by_row, by_col):
    total = parts[0][0:1, 0:1]
    for part in parts[1:]:
        total = total + part[0:1, 0:1]
    clip = jnp.maximum(1.0, jnp.sqrt(total / elements))
    return by_row[...] / clip, by_col[...]


def fresh_kernel(n, elements, grads, weight, row_factor, col_factor, *refs):
    parts, outs = refs[:n], refs[n:]
    by_row, by_col = factors(elements, parts, row_factor, col_factor)
    n_chunks, chunk = by_row.shape
    cols = grads.shape[1]
    for j in range(n_chunks):
        column = as_column(by_row[j : j + 1])
        for k in range(cols // 128):
            at = slice(j * chunk, (j + 1) * chunk), slice(k * 128, (k + 1) * 128)
            update = grads[at] * column * by_col[:, k * 128 : (k + 1) * 128]
            fresh = (weight[at] - learn_rate * update).astype(jnp.bfloat16)
            split = outs[0].shape[0]
            low, high = j * chunk, (j + 1) * chunk
            if low < split:
                outs[0][low : min(high, split), at[1]] = fresh[: min(high, split) - low]
            if high > split:
                first = max(low, split)
                outs[1][first - split : high - split, at[1]] = fresh[first - low :]


def update_kernel(n, elements, grads, row_factor, col_factor, *refs):
    parts, out = refs[:n], refs[n]
    by_row, by_col = factors(elements, parts, row_factor, col_factor)
    n_chunks, chunk = by_row.shape
    for j in range(n_chunks):
        column = as_column(by_row[j : j + 1])
        for k in range(grads.shape[1] // 128):
            at = slice(j * chunk, (j + 1) * chunk), slice(k * 128, (k + 1) * 128)
            out[at] = grads[at] * column * by_col[:, k * 128 : (k + 1) * 128]


def place_kernel(entries, table, *refs):
    pieces, out, sems = refs[: len(entries)], refs[-2], refs[-1]
    copies = []
    for k, piece in enumerate(pieces):
        at = pl.ds(pl.multiple_of(table[entries[k]], 16), piece.shape[0])
        copies.append(pltpu.make_async_copy(piece, out.at[at], sems.at[k]))
    for copy in copies:
        copy.start()
    for copy in copies:
        copy.wait()


SCALARS = pl.BlockSpec(memory_space=pltpu.SMEM)
FAR = pl.BlockSpec(memory_space=pltpu.HBM)
ANYWHERE = pl.BlockSpec(memory_space=pl.ANY)
NEAR = pl.BlockSpec(memory_space=pltpu.VMEM)


def call(kernel, out_shape, *args, flops=0, specs=None, moved=None, **more):
    outs = out_shape if isinstance(out_shape, (tuple, list)) else [out_shape]
    if moved is None:
        moved = sum(x.size * x.dtype.itemsize for x in [*args, *outs])
    return pl.pallas_call(
        kernel,
        out_shape=out_shape,
        in_specs=specs or [NEAR] * len(args),
        compiler_params=pltpu.CompilerParams(vmem_limit_bytes=VMEM_LIMIT),
        cost_estimate=pl.CostEstimate(flops=flops, bytes_accessed=moved, transcendentals=0),
        **more,
    )(*args)


def shape_of(*dims, dtype=jnp.float32):
    return jax.ShapeDtypeStruct(dims, dtype)


def slices(hidden, table, entries, rows):
    n = len(entries)
    if rows % 128:
        return [lax.dynamic_slice_in_dim(hidden, table[e], rows, axis=1) for e in entries]
    shapes = [shape_of(hidden.shape[0], rows, dtype=hidden.dtype)] * n
    return call(
        functools.partial(slice_kernel, entries),
        shapes,
        table,
        hidden,
        specs=[SCALARS, FAR],
        moved=4 * n * hidden.shape[0] * rows,
        scratch_shapes=[pltpu.SemaphoreType.DMA((n,))],
    )


def product(hidden, table, entry, rows, peers, gs, coded, bases=(), light=False):
    half = gs[0].shape[1] // 2
    shapes = [
        shape_of(rows + TAIL, half, dtype=jnp.bfloat16) if c else shape_of(rows, half) for c in coded
    ]
    copied = entry is not None and rows % 128 == 0
    hs, source, scratch = list(peers), [], []
    if copied:
        source = [table, hidden]
        held = pltpu.VMEM((hidden.shape[0], rows), hidden.dtype)
        scratch = [held, pltpu.SemaphoreType.DMA((len(pieces_of(rows)),))]
    elif entry is not None:
        hs = slices(hidden, table, [entry], rows) + hs
    flops = sum(2 * g.size * rows for g in gs)
    rest = [*hs, *gs, *bases]
    moved = sum(x.size * x.dtype.itemsize for x in rest + shapes)
    if light:
        flops, moved = 0, 1
    return call(
        functools.partial(product_kernel, (int(copied), len(hs), len(bases)), entry, coded),
        shapes,
        *source,
        *rest,
        flops=flops,
        specs=[SCALARS, FAR][: len(source)] + [NEAR] * len(rest),
        moved=moved,
        scratch_shapes=scratch,
    )


def relay(base, messages):
    rows, half = base.shape
    shape = shape_of(rows + TAIL, half, dtype=jnp.bfloat16)
    return call(functools.partial(relay_kernel, len(messages)), shape, base, *messages)


def gather(base, messages):
    if not messages:
        return base
    shape = shape_of(*base.shape)
    return call(functools.partial(gather_kernel, len(messages)), shape, base, *messages)


def final(bases, first, second):
    rows, half = bases[0].shape
    chunk = chunk_of(rows)
    shapes = [shape_of(rows, 2 * half), shape_of(rows // chunk, chunk), shape_of(1, 2 * half)]
    kernel = functools.partial(final_kernel, (len(first), len(second)))
    return call(kernel, shapes, *bases, *first, *second)


def place(pieces, table, entries, out):
    n = len(pieces)
    old = [] if isinstance(out, jax.ShapeDtypeStruct) else [out]
    return call(
        functools.partial(place_kernel, entries),
        jax.ShapeDtypeStruct(out.shape, out.dtype),
        table,
        *pieces,
        *old,
        specs=[SCALARS] + [NEAR] * n + [ANYWHERE] * len(old),
        moved=sum(4 * p.size for p in pieces),
        out_specs=ANYWHERE,
        scratch_shapes=[pltpu.SemaphoreType.DMA((n,))],
        input_output_aliases={n + 1: 0} if old else {},
    )


def after(x, *others):
    return lax.optimization_barrier((x, others))[0]


def grid_of(seq):
    hi = int(math.isqrt(seq))
    while seq % hi:
        hi -= 1
    return hi, seq // hi


def solution(mesh):
    n_dp, n_seq, n_tensor = (mesh.shape[name] for name in ("dp", "seq", "tensor"))
    n_hi, n_lo = grid_of(n_seq)
    his, los = range(1, n_hi), range(1, n_lo)

    def shift(x, hi=0, lo=0):
        pairs = [
            (a * n_lo + b, (a + hi) % n_hi * n_lo + (b + lo) % n_lo)
            for a in range(n_hi)
            for b in range(n_lo)
        ]
        return lax.ppermute(x, "seq", pairs)

    def turn(x, axis, n, step):
        return lax.ppermute(x, axis, [(a, (a + step) % n) for a in range(n)])

    def exchange(parts, axis, n, step=None):
        step = step or (lambda x, d: turn(x, axis, n, d))
        if axis is not None and n & (n - 1) == 0:
            d = 1
            while d < n:
                x = sum(parts[1:], parts[0])
                parts = [x, lax.ppermute(x, axis, [(a, a ^ d) for a in range(n)])]
                d *= 2
            return parts
        if n == 1:
            return parts
        x = sum(parts[1:], parts[0])
        return [x] + [step(x, d) for d in range(1, n)]

    def per_device(hidden, grad_out, master_weight, row_prev, col_prev):
        rows, cols = master_weight.shape

        def settle(x):
            return x if rows % 128 else pltpu.with_memory_space_constraint(x, pltpu.HBM)

        given, hidden = hidden, settle(hidden)
        all_rows, all_cols = rows * n_dp * n_seq, cols * n_tensor
        dp, seq = lax.axis_index("dp"), lax.axis_index("seq")
        my_hi, my_lo = seq // n_lo, seq % n_lo

        part_rows = rows // 2
        cells = np.array([(p, hi, lo) for p in range(n_dp) for hi in range(n_hi) for lo in range(n_lo)])
        places = np.array([(hi, lo, k) for hi in range(n_hi) for lo in range(n_lo) for k in (0, 1)])

        def block_of(hi, lo):
            return lax.rem(my_hi + hi, n_hi) * n_lo + lax.rem(my_lo + lo, n_lo)

        p, hi, lo = (jnp.asarray(x, jnp.int32) for x in cells.T)
        columns = (lax.rem(dp + p, n_dp) * n_seq + block_of(hi, lo)) * rows
        hi, lo, k = (jnp.asarray(x, jnp.int32) for x in places.T)
        table = block_of(n_hi - hi, n_lo - lo) * rows + k * part_rows
        table = jnp.concatenate([columns, table])

        def start_of(p, hi, lo):
            return (p * n_hi + hi) * n_lo + lo

        def row_of(part, hi, lo):
            return len(cells) + (hi * n_lo + lo) * 2 + part

        def peers_of(group, source):
            found = {at: [] for at in group}
            for p in range(1, n_dp if group else 1):
                entries = [start_of(p, *at) for at in group]
                for at, block in zip(group, slices(source, table, entries, rows)):
                    found[at].append(turn(block, "dp", n_dp, p))
            return found

        gs = [grad_out] + [turn(grad_out, "dp", n_dp, p) for p in range(1, n_dp)]
        far_group = [(hi, lo) for hi in his for lo in los]
        near_group = [(0, lo) for lo in los] + [(hi, 0) for hi in his] + [(0, 0)]
        blocks = peers_of(far_group, hidden)

        far, sent = [{}, {}], []
        for hi, lo in far_group:
            bases = product(hidden, table, start_of(0, hi, lo), rows, [], gs[:1], (False, False))
            if n_dp > 1:
                coded = product(None, None, None, rows, blocks[hi, lo], gs[1:], (True, True), bases)
            else:
                coded = [relay(x, []) for x in bases]
            sent += coded
            far[0][hi, lo] = shift(coded[0], lo=lo)
            far[1][hi, lo] = shift(coded[1], hi=hi)

        hidden = settle(after(given, *sent))
        blocks = peers_of(near_group, hidden)

        def whole_product(hi, lo, coded):
            entry = start_of(0, hi, lo)
            return product(hidden, table, entry, rows, blocks[hi, lo], gs, coded, light=True)

        near, base = [{}, {}], [{}, {}]
        for lo in los:
            first, base[1][lo] = whole_product(0, lo, (True, False))
            near[0][lo] = shift(first, lo=lo)
        for hi in his:
            base[0][hi], second = whole_product(hi, 0, (False, True))
            near[1][hi] = shift(second, hi=hi)
        own = whole_product(0, 0, (False, False))
        last = [{}, {}]
        for hi in his:
            message = relay(base[0][hi], [far[0][hi, lo] for lo in los])
            last[0][hi] = shift(message, hi=hi)
        for lo in los:
            message = relay(base[1][lo], [far[1][hi, lo] for hi in his])
            last[1][lo] = shift(message, lo=lo)
        own = [gather(own[part], list(near[part].values())) for part in (0, 1)]
        grads, row_part, col_part = final(own, list(last[0].values()), list(last[1].values()))

        chunks = row_part.shape
        parts = exchange([row_part], "tensor", n_tensor)
        new_rows, by_row, both = call(
            functools.partial(rows_kernel, len(parts), all_cols),
            [shape_of(*chunks), shape_of(*chunks), shape_of(2, cols)],
            grads,
            row_prev.reshape(chunks),
            col_part,
            *parts,
        )
        parts = exchange([both], "dp", n_dp)
        parts = exchange(parts, None, n_lo, lambda x, d: shift(x, lo=d))
        parts = exchange(parts, None, n_hi, lambda x, d: shift(x, hi=d))
        new_cols, by_col, share = call(
            functools.partial(cols_kernel, len(parts), all_rows),
            [shape_of(1, cols), shape_of(1, cols), shape_of(1, 128)],
            col_prev.reshape(1, cols),
            *parts,
        )
        parts = exchange([share], "tensor", n_tensor)
        elements = all_rows * all_cols

        pair = call(
            functools.partial(fresh_kernel, len(parts), elements),
            [shape_of(part_rows, cols, dtype=jnp.bfloat16)] * 2,
            grads,
            master_weight,
            by_row,
            by_col,
            *parts,
        )
        along_lo, along_hi = {}, {}
        for lo in los:
            along_lo[0, lo] = shift(pair[0], lo=lo)
        for hi in his:
            along_hi[1, hi] = shift(pair[1], hi=hi)
        for lo in los:
            along_lo[1, lo] = shift(pair[1], lo=lo)
        for hi in his:
            along_hi[0, hi] = shift(pair[0], hi=hi)

        onward = []
        for hi in his:
            for lo in los:
                onward.append((shift(along_lo[0, lo], hi=hi), row_of(0, hi, lo)))
                onward.append((shift(along_hi[1, hi], lo=lo), row_of(1, hi, lo)))
        update = call(
            functools.partial(update_kernel, len(parts), elements),
            shape_of(rows, cols),
            after(grads, *along_lo.values()),
            by_row,
            by_col,
            *parts,
        )

        whole = jax.ShapeDtypeStruct((rows * n_seq, cols), jnp.bfloat16)
        new_weight = place(pair, table, [row_of(part, 0, 0) for part in (0, 1)], whole)
        pieces = [(x, row_of(part, 0, lo)) for (part, lo), x in along_lo.items()]
        pieces += [(x, row_of(part, hi, 0)) for (part, hi), x in along_hi.items()]
        for group in (pieces, onward):
            if group:
                new_weight = place([x for x, _ in group], table, [e for _, e in group], new_weight)
        return (new_weight, update, new_rows.reshape(rows), new_cols.reshape(cols))

    return jax.shard_map(
        per_device,
        mesh=mesh,
        in_specs=(
            P(("dp", "seq"), None),
            P(("dp", "seq"), "tensor"),
            P(("dp", "seq"), "tensor"),
            P(("dp", "seq")),
            P("tensor"),
        ),
        out_specs=(P("dp", "tensor"), P(("dp", "seq"), "tensor"), P(("dp", "seq")), P("tensor")),
        check_vma=False,
    )
```

```python
import functools
import math

import jax
import jax.numpy as jnp
from jax import lax
from jax.experimental import pallas as pl
from jax.experimental.pallas import tpu as pltpu
from jax.sharding import PartitionSpec as P

decay_rate = 0.8
learn_rate = 0.05
small_term = 1e-06

POWER = 11
TOP = 2.0 ** (125.0 / POWER)
TAIL = 16
VMEM_LIMIT = 16 * 2**20


def chunk_of(rows):
    return 128 if rows % 128 == 0 else rows


def encode(x):
    top = jnp.max(jnp.abs(x), axis=0, keepdims=True)
    scale = jnp.maximum(top * 1.004, 1e-30).astype(jnp.bfloat16).astype(jnp.float32)
    u = x * (TOP / scale)
    u2 = u * u
    u4 = u2 * u2
    return (u4 * u4 * u2 * u).astype(jnp.bfloat16), scale


def decode(code, scale):
    code = code.astype(jnp.float32)
    size = jnp.abs(code)
    u = jnp.exp(jnp.log(jnp.maximum(size, 1e-37)) * (1.0 / POWER)) * (scale * (1.0 / TOP))
    return jnp.where(size > 1e-37, jnp.where(code > 0, u, -u), 0.0)


def write_scales(ref, scales):
    rows, cols = ref.shape
    at = lax.broadcasted_iota(jnp.int32, (TAIL, cols), 0)
    tail = jnp.zeros((TAIL, cols), jnp.float32)
    for j, scale in enumerate(scales):
        tail = jnp.where(at == j, scale, tail)
    ref[rows - TAIL :] = tail.astype(jnp.bfloat16)


def read_scales(ref):
    return ref[ref.shape[0] - TAIL :].astype(jnp.float32)


def product_kernel(layout, start_of, coded, *refs):
    placed, n_hs, n_base = layout
    refs = list(refs)
    take = lambda k: [refs.pop(0) for _ in range(k)]
    hs, gs, bases, outs = take(n_hs), take(n_hs), take(n_base), refs
    cols = gs[0].shape[1]
    rows = outs[0].shape[0] - (TAIL if coded[0] else 0)
    half, chunk = cols // 2, chunk_of(rows)
    first = [start_of() if k == 0 and placed else 0 for k in range(n_hs)]
    scales = [[], []]
    for j in range(rows // chunk):
        at = slice(j * chunk, (j + 1) * chunk)
        total = None
        for k, (h, g) in enumerate(zip(hs, gs)):
            if k == 0 and placed:
                block = h[:, pl.ds(pl.multiple_of(first[k] + j * chunk, chunk), chunk)]
            else:
                block = h[:, at]
            term = lax.dot_general(
                block, g[...], (((0,), (0,)), ((), ())), preferred_element_type=jnp.float32
            )
            total = term if total is None else total + term
        for part in (0, 1):
            x = total[:, part * half : (part + 1) * half]
            if bases:
                x = x + bases[part][at]
            if coded[part]:
                outs[part][at], scale = encode(x)
                scales[part].append(scale)
            else:
                outs[part][at] = x
    for part in (0, 1):
        if coded[part]:
            write_scales(outs[part], scales[part])


LOADS = 4


def load_kernel(starts_of, hidden, held, *refs):
    outs, sems = refs[:-1], refs[-1]
    step = hidden.shape[0] // LOADS
    copies = []
    for k in range(LOADS):
        at = pl.ds(k * step, step)
        copies.append(pltpu.make_async_copy(hidden.at[at], held.at[at], sems.at[k]))
        copies[k].start()
    starts = [pl.multiple_of(start_of(), 128) for start_of in starts_of]
    for k in range(LOADS):
        copies[k].wait()
        for start, out in zip(starts, outs):
            at = slice(k * step, (k + 1) * step)
            out[at] = held[at, pl.ds(start, out.shape[1])]


def relay_kernel(n, base, *refs):
    messages, out = refs[:n], refs[n]
    rows = base.shape[0]
    chunk = chunk_of(rows)
    tails = [read_scales(m) for m in messages]
    scales = []
    for j in range(rows // chunk):
        at = slice(j * chunk, (j + 1) * chunk)
        total = base[at]
        for m, tail in zip(messages, tails):
            total = total + decode(m[at], tail[j : j + 1])
        out[at], scale = encode(total)
        scales.append(scale)
    write_scales(out, scales)


def gather_kernel(n, base, *refs):
    messages, out = refs[:n], refs[n]
    rows = base.shape[0]
    chunk = chunk_of(rows)
    tails = [read_scales(m) for m in messages]
    for j in range(rows // chunk):
        at = slice(j * chunk, (j + 1) * chunk)
        total = base[at]
        for m, tail in zip(messages, tails):
            total = total + decode(m[at], tail[j : j + 1])
        out[at] = total


def final_kernel(counts, *refs):
    bases, refs = refs[:2], refs[2:]
    messages = refs[: counts[0]], refs[counts[0] : sum(counts)]
    out, row_out, col_out = refs[sum(counts) :]
    rows, half = bases[0].shape
    chunk = chunk_of(rows)
    tails = [[read_scales(m) for m in group] for group in messages]
    col_sums = [jnp.zeros((1, half), jnp.float32)] * 2
    for j in range(rows // chunk):
        at = slice(j * chunk, (j + 1) * chunk)
        row_sum = jnp.zeros((chunk, 128), jnp.float32)
        for part in (0, 1):
            total = bases[part][at]
            for m, tail in zip(messages[part], tails[part]):
                total = total + decode(m[at], tail[j : j + 1])
            out[at, part * half : (part + 1) * half] = total
            squares = total * total
            col_sums[part] = col_sums[part] + jnp.sum(squares, axis=0, keepdims=True)
            for k in range(half // 128):
                row_sum = row_sum + squares[:, k * 128 : (k + 1) * 128]
        row_out[j : j + 1] = jnp.sum(row_sum.T, axis=0, keepdims=True)
    for part in (0, 1):
        col_out[:, part * half : (part + 1) * half] = col_sums[part]


def as_column(row):
    return jnp.broadcast_to(row, (128, row.shape[1])).T


def rows_kernel(n, all_cols, grads, row_prev, col_part, *refs):
    parts, (rows_out, by_row_out, both_out) = refs[:n], refs[n:]
    total = sum(p[...] for p in parts[1:]) + parts[0][...] if n > 1 else parts[0][...]
    total = total + small_term * all_cols
    new_rows = decay_rate * row_prev[...] + (1.0 - decay_rate) * total / all_cols
    rows_out[...] = new_rows
    by_row_out[...] = 1.0 / jnp.sqrt(new_rows)
    inverse = 1.0 / new_rows
    n_chunks, chunk = new_rows.shape
    cols = grads.shape[1]
    sums = [jnp.zeros((1, 128), jnp.float32)] * (cols // 128)
    for j in range(n_chunks):
        weight = as_column(inverse[j : j + 1])
        for k in range(cols // 128):
            g = grads[j * chunk : (j + 1) * chunk, k * 128 : (k + 1) * 128]
            sums[k] = sums[k] + jnp.sum(g * g * weight, axis=0, keepdims=True)
    both_out[0:1] = col_part[...]
    for k in range(cols // 128):
        both_out[1:2, k * 128 : (k + 1) * 128] = sums[k]


def cols_kernel(n, all_rows, col_prev, *refs):
    parts, (cols_out, by_col_out, total_out) = refs[:n], refs[n:]
    both = sum(p[...] for p in parts[1:]) + parts[0][...] if n > 1 else parts[0][...]
    total = both[0:1] + small_term * all_rows
    new_cols = decay_rate * col_prev[...] + (1.0 - decay_rate) * total / all_rows
    cols_out[...] = new_cols
    by_col_out[...] = 1.0 / jnp.sqrt(new_cols)
    share = jnp.sum(both[1:2] / new_cols, axis=1, keepdims=True)
    total_out[...] = jnp.broadcast_to(share, total_out.shape)


def factors(elements, parts, by_row, by_col):
    total = parts[0][0:1, 0:1]
    for part in parts[1:]:
        total = total + part[0:1, 0:1]
    clip = jnp.maximum(1.0, jnp.sqrt(total / elements))
    return by_row[...] / clip, by_col[...]


def fresh_kernel(n, elements, grads, weight, row_factor, col_factor, *refs):
    parts, outs = refs[:n], refs[n:]
    by_row, by_col = factors(elements, parts, row_factor, col_factor)
    n_chunks, chunk = by_row.shape
    cols = grads.shape[1]
    for j in range(n_chunks):
        column = as_column(by_row[j : j + 1])
        for k in range(cols // 128):
            at = slice(j * chunk, (j + 1) * chunk), slice(k * 128, (k + 1) * 128)
            update = grads[at] * column * by_col[:, k * 128 : (k + 1) * 128]
            fresh = (weight[at] - learn_rate * update).astype(jnp.bfloat16)
            split = outs[0].shape[0]
            low, high = j * chunk, (j + 1) * chunk
            if low < split:
                outs[0][low : min(high, split), at[1]] = fresh[: min(high, split) - low]
            if high > split:
                first = max(low, split)
                outs[1][first - split : high - split, at[1]] = fresh[first - low :]


def update_kernel(n, elements, grads, row_factor, col_factor, *refs):
    parts, out = refs[:n], refs[n]
    by_row, by_col = factors(elements, parts, row_factor, col_factor)
    n_chunks, chunk = by_row.shape
    for j in range(n_chunks):
        column = as_column(by_row[j : j + 1])
        for k in range(grads.shape[1] // 128):
            at = slice(j * chunk, (j + 1) * chunk), slice(k * 128, (k + 1) * 128)
            out[at] = grads[at] * column * by_col[:, k * 128 : (k + 1) * 128]


def place_kernel(rows_of, *refs):
    pieces, out, sems = refs[: len(rows_of)], refs[-2], refs[-1]
    copies = []
    for k, piece in enumerate(pieces):
        at = pl.ds(pl.multiple_of(rows_of[k](), 16), piece.shape[0])
        copies.append(pltpu.make_async_copy(piece, out.at[at], sems.at[k]))
    for copy in copies:
        copy.start()
    for copy in copies:
        copy.wait()


FAR = pl.BlockSpec(memory_space=pltpu.HBM)
ANYWHERE = pl.BlockSpec(memory_space=pl.ANY)
NEAR = pl.BlockSpec(memory_space=pltpu.VMEM)


def call(kernel, out_shape, *args, flops=0, specs=None, moved=None, **more):
    outs = out_shape if isinstance(out_shape, (tuple, list)) else [out_shape]
    if moved is None:
        moved = sum(x.size * x.dtype.itemsize for x in [*args, *outs])
    return pl.pallas_call(
        kernel,
        out_shape=out_shape,
        in_specs=specs or [NEAR] * len(args),
        compiler_params=pltpu.CompilerParams(vmem_limit_bytes=VMEM_LIMIT),
        cost_estimate=pl.CostEstimate(flops=flops, bytes_accessed=moved, transcendentals=0),
        **more,
    )(*args)


def shape_of(*dims, dtype=jnp.float32):
    return jax.ShapeDtypeStruct(dims, dtype)


def load(hidden, starts_of, rows):
    if rows % 128 or hidden.shape[0] % (16 * LOADS):
        return hidden, [lax.dynamic_slice_in_dim(hidden, f(), rows, axis=1) for f in starts_of]
    shapes = [shape_of(hidden.shape[0], rows, dtype=hidden.dtype)] * len(starts_of)
    held, *blocks = call(
        functools.partial(load_kernel, starts_of),
        [jax.ShapeDtypeStruct(hidden.shape, hidden.dtype)] + shapes,
        pltpu.with_memory_space_constraint(hidden, pltpu.HBM),
        specs=[FAR],
        moved=4 * hidden.size,
        scratch_shapes=[pltpu.SemaphoreType.DMA((LOADS,))],
    )
    return held, blocks


def product(held, start_of, rows, peers, gs, coded, bases=(), light=False):
    half = gs[0].shape[1] // 2
    shapes = [
        shape_of(rows + TAIL, half, dtype=jnp.bfloat16) if c else shape_of(rows, half) for c in coded
    ]
    placed = start_of is not None and rows % 128 == 0
    hs = list(peers)
    if placed:
        hs = [held] + hs
    elif start_of is not None:
        hs = [lax.dynamic_slice_in_dim(held, start_of(), rows, axis=1)] + hs
    flops = sum(2 * g.size * rows for g in gs)
    moved = sum(x.size * x.dtype.itemsize for x in [*gs, *bases, *shapes])
    if light:
        flops, moved = 0, 1
    return call(
        functools.partial(product_kernel, (placed, len(hs), len(bases)), start_of, coded),
        shapes,
        *hs,
        *gs,
        *bases,
        flops=flops,
        moved=moved,
    )


def relay(base, messages):
    rows, half = base.shape
    shape = shape_of(rows + TAIL, half, dtype=jnp.bfloat16)
    return call(functools.partial(relay_kernel, len(messages)), shape, base, *messages)


def gather(base, messages):
    if not messages:
        return base
    shape = shape_of(*base.shape)
    return call(functools.partial(gather_kernel, len(messages)), shape, base, *messages)


def final(bases, first, second):
    rows, half = bases[0].shape
    chunk = chunk_of(rows)
    shapes = [shape_of(rows, 2 * half), shape_of(rows // chunk, chunk), shape_of(1, 2 * half)]
    kernel = functools.partial(final_kernel, (len(first), len(second)))
    return call(kernel, shapes, *bases, *first, *second)


def place(pieces, rows_of, out):
    n = len(pieces)
    old = [] if isinstance(out, jax.ShapeDtypeStruct) else [out]
    return call(
        functools.partial(place_kernel, rows_of),
        jax.ShapeDtypeStruct(out.shape, out.dtype),
        *pieces,
        *old,
        specs=[NEAR] * n + [ANYWHERE] * len(old),
        moved=sum(4 * p.size for p in pieces),
        out_specs=ANYWHERE,
        scratch_shapes=[pltpu.SemaphoreType.DMA((n,))],
        input_output_aliases={n: 0} if old else {},
    )


def after(x, *others):
    return lax.optimization_barrier((x, others))[0]


def grid_of(seq):
    hi = int(math.isqrt(seq))
    while seq % hi:
        hi -= 1
    return hi, seq // hi


def solution(mesh):
    n_dp, n_seq, n_tensor = (mesh.shape[name] for name in ("dp", "seq", "tensor"))
    n_hi, n_lo = grid_of(n_seq)
    his, los = range(1, n_hi), range(1, n_lo)

    def shift(x, hi=0, lo=0):
        pairs = [
            (a * n_lo + b, (a + hi) % n_hi * n_lo + (b + lo) % n_lo)
            for a in range(n_hi)
            for b in range(n_lo)
        ]
        return lax.ppermute(x, "seq", pairs)

    def turn(x, axis, n, step):
        return lax.ppermute(x, axis, [(a, (a + step) % n) for a in range(n)])

    def exchange(parts, axis, n, step=None):
        step = step or (lambda x, d: turn(x, axis, n, d))
        if axis is not None and n & (n - 1) == 0:
            d = 1
            while d < n:
                x = sum(parts[1:], parts[0])
                parts = [x, lax.ppermute(x, axis, [(a, a ^ d) for a in range(n)])]
                d *= 2
            return parts
        if n == 1:
            return parts
        x = sum(parts[1:], parts[0])
        return [x] + [step(x, d) for d in range(1, n)]

    def per_device(hidden, grad_out, master_weight, row_prev, col_prev):
        rows, cols = master_weight.shape

        part_rows = rows // 2
        all_rows, all_cols = rows * n_dp * n_seq, cols * n_tensor

        def block_of(hi, lo):
            seq = lax.axis_index("seq")
            mine = lax.div(seq, n_lo), lax.rem(seq, n_lo)
            return lax.rem(mine[0] + hi, n_hi) * n_lo + lax.rem(mine[1] + lo, n_lo)

        def start_of(p, hi, lo):
            return lambda: (
                lax.rem(lax.axis_index("dp") + p, n_dp) * n_seq + block_of(hi, lo)
            ) * rows

        def row_of(part, hi, lo):
            return lambda: block_of(n_hi - hi, n_lo - lo) * rows + part * part_rows

        gs = [grad_out] + [turn(grad_out, "dp", n_dp, p) for p in range(1, n_dp)]
        far_group = [(hi, lo) for hi in his for lo in los]
        near_group = [(0, lo) for lo in los] + [(hi, 0) for hi in his] + [(0, 0)]
        keys = [(p, at) for at in far_group + near_group for p in range(1, n_dp)]
        held, sent = load(hidden, [start_of(p, *at) for p, at in keys], rows)
        blocks = {at: [] for at in far_group + near_group}
        for (p, at), block in zip(keys, sent):
            blocks[at].append(turn(block, "dp", n_dp, p))

        far = [{}, {}]
        for hi, lo in far_group:
            bases = product(held, start_of(0, hi, lo), rows, [], gs[:1], (False, False))
            if n_dp > 1:
                coded = product(None, None, rows, blocks[hi, lo], gs[1:], (True, True), bases)
            else:
                coded = [relay(x, []) for x in bases]
            far[0][hi, lo] = shift(coded[0], lo=lo)
            far[1][hi, lo] = shift(coded[1], hi=hi)

        def whole_product(hi, lo, coded):
            peers = blocks[hi, lo]
            return product(held, start_of(0, hi, lo), rows, peers, gs, coded, light=True)

        near, base = [{}, {}], [{}, {}]
        for lo in los:
            first, base[1][lo] = whole_product(0, lo, (True, False))
            near[0][lo] = shift(first, lo=lo)
        for hi in his:
            base[0][hi], second = whole_product(hi, 0, (False, True))
            near[1][hi] = shift(second, hi=hi)
        own = whole_product(0, 0, (False, False))
        last = [{}, {}]
        for hi in his:
            message = relay(base[0][hi], [far[0][hi, lo] for lo in los])
            last[0][hi] = shift(message, hi=hi)
        for lo in los:
            message = relay(base[1][lo], [far[1][hi, lo] for hi in his])
            last[1][lo] = shift(message, lo=lo)
        own = [gather(own[part], list(near[part].values())) for part in (0, 1)]
        grads, row_part, col_part = final(own, list(last[0].values()), list(last[1].values()))

        chunks = row_part.shape
        parts = exchange([row_part], "tensor", n_tensor)
        new_rows, by_row, both = call(
            functools.partial(rows_kernel, len(parts), all_cols),
            [shape_of(*chunks), shape_of(*chunks), shape_of(2, cols)],
            grads,
            row_prev.reshape(chunks),
            col_part,
            *parts,
        )
        parts = exchange([both], "dp", n_dp)
        parts = exchange(parts, None, n_lo, lambda x, d: shift(x, lo=d))
        parts = exchange(parts, None, n_hi, lambda x, d: shift(x, hi=d))
        new_cols, by_col, share = call(
            functools.partial(cols_kernel, len(parts), all_rows),
            [shape_of(1, cols), shape_of(1, cols), shape_of(1, 128)],
            col_prev.reshape(1, cols),
            *parts,
        )
        parts = exchange([share], "tensor", n_tensor)
        elements = all_rows * all_cols

        pair = call(
            functools.partial(fresh_kernel, len(parts), elements),
            [shape_of(part_rows, cols, dtype=jnp.bfloat16)] * 2,
            grads,
            master_weight,
            by_row,
            by_col,
            *parts,
        )
        along_lo, along_hi = {}, {}
        for lo in los:
            along_lo[0, lo] = shift(pair[0], lo=lo)
        for hi in his:
            along_hi[1, hi] = shift(pair[1], hi=hi)
        for lo in los:
            along_lo[1, lo] = shift(pair[1], lo=lo)
        for hi in his:
            along_hi[0, hi] = shift(pair[0], hi=hi)

        onward = []
        for hi in his:
            for lo in los:
                onward.append((shift(along_lo[0, lo], hi=hi), row_of(0, hi, lo)))
                onward.append((shift(along_hi[1, hi], lo=lo), row_of(1, hi, lo)))
        update = call(
            functools.partial(update_kernel, len(parts), elements),
            shape_of(rows, cols),
            after(grads, *along_lo.values()),
            by_row,
            by_col,
            *parts,
        )

        whole = jax.ShapeDtypeStruct((rows * n_seq, cols), jnp.bfloat16)
        new_weight = place(pair, [row_of(part, 0, 0) for part in (0, 1)], whole)
        pieces = [(x, row_of(part, 0, lo)) for (part, lo), x in along_lo.items()]
        pieces += [(x, row_of(part, hi, 0)) for (part, hi), x in along_hi.items()]
        for group in (pieces, onward):
            if group:
                new_weight = place([x for x, _ in group], [f for _, f in group], new_weight)
        return (new_weight, update, new_rows.reshape(rows), new_cols.reshape(cols))

    return jax.shard_map(
        per_device,
        mesh=mesh,
        in_specs=(
            P(("dp", "seq"), None),
            P(("dp", "seq"), "tensor"),
            P(("dp", "seq"), "tensor"),
            P(("dp", "seq")),
            P("tensor"),
        ),
        out_specs=(P("dp", "tensor"), P(("dp", "seq"), "tensor"), P(("dp", "seq")), P("tensor")),
        check_vma=False,
    )
```

```python
import functools
import math

import jax
import jax.numpy as jnp
from jax import lax
from jax.experimental import pallas as pl
from jax.experimental.pallas import tpu as pltpu
from jax.sharding import PartitionSpec as P

decay_rate = 0.8
learn_rate = 0.05
small_term = 1e-06

POWER = 11
TOP = 2.0 ** (125.0 / POWER)
TAIL = 16
VMEM_LIMIT = 16 * 2**20


def chunk_of(rows):
    return 128 if rows % 128 == 0 else rows


def encode(x):
    top = jnp.max(jnp.abs(x), axis=0, keepdims=True)
    scale = jnp.maximum(top * 1.004, 1e-30).astype(jnp.bfloat16).astype(jnp.float32)
    u = x * (TOP / scale)
    u2 = u * u
    u4 = u2 * u2
    return (u4 * u4 * u2 * u).astype(jnp.bfloat16), scale


def decode(code, scale):
    code = code.astype(jnp.float32)
    size = jnp.abs(code)
    u = jnp.exp(jnp.log(jnp.maximum(size, 1e-37)) * (1.0 / POWER)) * (scale * (1.0 / TOP))
    return jnp.where(size > 1e-37, jnp.where(code > 0, u, -u), 0.0)


def write_scales(ref, scales):
    rows, cols = ref.shape
    at = lax.broadcasted_iota(jnp.int32, (TAIL, cols), 0)
    tail = jnp.zeros((TAIL, cols), jnp.float32)
    for j, scale in enumerate(scales):
        tail = jnp.where(at == j, scale, tail)
    ref[rows - TAIL :] = tail.astype(jnp.bfloat16)


def read_scales(ref):
    return ref[ref.shape[0] - TAIL :].astype(jnp.float32)


def product_kernel(layout, start_of, coded, *refs):
    placed, n_hs, n_base = layout
    refs = list(refs)
    take = lambda k: [refs.pop(0) for _ in range(k)]
    hs, gs, bases, outs = take(n_hs), take(n_hs), take(n_base), refs
    cols = gs[0].shape[1]
    rows = outs[0].shape[0] - (TAIL if coded[0] else 0)
    half, chunk = cols // 2, chunk_of(rows)
    first = [start_of() if k == 0 and placed else 0 for k in range(n_hs)]
    scales = [[], []]
    for j in range(rows // chunk):
        at = slice(j * chunk, (j + 1) * chunk)
        total = None
        for k, (h, g) in enumerate(zip(hs, gs)):
            if k == 0 and placed:
                block = h[:, pl.ds(pl.multiple_of(first[k] + j * chunk, chunk), chunk)]
            else:
                block = h[:, at]
            term = lax.dot_general(
                block, g[...], (((0,), (0,)), ((), ())), preferred_element_type=jnp.float32
            )
            total = term if total is None else total + term
        for part in (0, 1):
            x = total[:, part * half : (part + 1) * half]
            if bases:
                x = x + bases[part][at]
            if coded[part]:
                outs[part][at], scale = encode(x)
                scales[part].append(scale)
            else:
                outs[part][at] = x
    for part in (0, 1):
        if coded[part]:
            write_scales(outs[part], scales[part])


def fetch_kernel(starts_of, hidden, grad_out, *refs):
    outs, grad_held, sems = refs[:-2], refs[-2], refs[-1]
    copies = []
    for k, (start_of, out) in enumerate(zip(starts_of, outs)):
        at = pl.ds(pl.multiple_of(start_of(), 128), out.shape[1])
        copies.append(pltpu.make_async_copy(hidden.at[:, at], out, sems.at[k]))
        copies[k].start()
    copies.append(pltpu.make_async_copy(grad_out, grad_held, sems.at[len(outs)]))
    copies[-1].start()
    for copy in copies:
        copy.wait()


def cut_kernel(starts_of, hidden, *outs):
    for start_of, out in zip(starts_of, outs):
        out[...] = hidden[:, pl.ds(pl.multiple_of(start_of(), 128), out.shape[1])]


def relay_kernel(n, base, *refs):
    messages, out = refs[:n], refs[n]
    rows = base.shape[0]
    chunk = chunk_of(rows)
    tails = [read_scales(m) for m in messages]
    scales = []
    for j in range(rows // chunk):
        at = slice(j * chunk, (j + 1) * chunk)
        total = base[at]
        for m, tail in zip(messages, tails):
            total = total + decode(m[at], tail[j : j + 1])
        out[at], scale = encode(total)
        scales.append(scale)
    write_scales(out, scales)


def gather_kernel(n, base, *refs):
    messages, out = refs[:n], refs[n]
    rows = base.shape[0]
    chunk = chunk_of(rows)
    tails = [read_scales(m) for m in messages]
    for j in range(rows // chunk):
        at = slice(j * chunk, (j + 1) * chunk)
        total = base[at]
        for m, tail in zip(messages, tails):
            total = total + decode(m[at], tail[j : j + 1])
        out[at] = total


def final_kernel(n, n_before, base, *refs):
    messages, refs = refs[:n], refs[n:]
    before, (out, row_out, col_out) = refs[:n_before], refs[n_before:]
    rows, half = base.shape
    chunk = chunk_of(rows)
    tails = [read_scales(m) for m in messages]
    col_sum = jnp.zeros((1, half), jnp.float32)
    for j in range(rows // chunk):
        at = slice(j * chunk, (j + 1) * chunk)
        row_sum = jnp.zeros((chunk, 128), jnp.float32)
        total = base[at]
        for m, tail in zip(messages, tails):
            total = total + decode(m[at], tail[j : j + 1])
        out[at] = total
        squares = total * total
        col_sum = col_sum + jnp.sum(squares, axis=0, keepdims=True)
        for k in range(half // 128):
            row_sum = row_sum + squares[:, k * 128 : (k + 1) * 128]
        row_sum = jnp.sum(row_sum.T, axis=0, keepdims=True)
        for row in before:
            row_sum = row_sum + row[j : j + 1]
        row_out[j : j + 1] = row_sum
    col_out[...] = col_sum


def columns_of(halves):
    half = halves[0].shape[1]
    for part in (0, 1):
        for k in range(0, half, 128):
            yield halves[part], slice(k, k + 128), slice(part * half + k, part * half + k + 128)


def as_column(row):
    return jnp.broadcast_to(row, (128, row.shape[1])).T


def tree_sum(terms):
    while len(terms) > 1:
        pairs = [sum(terms[k + 1 : k + 2], terms[k]) for k in range(0, len(terms), 2)]
        terms = pairs
    return terms[0]


def rows_kernel(n, all_cols, low, high, row_prev, low_col, high_col, *refs):
    parts, (rows_out, by_row_out, both_out) = refs[:n], refs[n:]
    total = tree_sum([p[...] for p in parts])
    total = total + small_term * all_cols
    new_rows = decay_rate * row_prev[...] + (1.0 - decay_rate) * total / all_cols
    rows_out[...] = new_rows
    by_row_out[...] = 1.0 / jnp.sqrt(new_rows)
    inverse = 1.0 / new_rows
    n_chunks, chunk = new_rows.shape
    half = low.shape[1]
    sums = [jnp.zeros((1, 128), jnp.float32)] * (2 * half // 128)
    for j in range(n_chunks):
        weight = as_column(inverse[j : j + 1])
        for k, (grads, at, _) in enumerate(columns_of((low, high))):
            g = grads[j * chunk : (j + 1) * chunk, at]
            sums[k] = sums[k] + jnp.sum(g * g * weight, axis=0, keepdims=True)
    both_out[0:1, :half] = low_col[...]
    both_out[0:1, half:] = high_col[...]
    for k, (_, _, there) in enumerate(columns_of((low, high))):
        both_out[1:2, there] = sums[k]


def cols_kernel(n, all_rows, col_prev, *refs):
    parts, (cols_out, by_col_out, total_out) = refs[:n], refs[n:]
    both = tree_sum([p[...] for p in parts])
    total = both[0:1] + small_term * all_rows
    new_cols = decay_rate * col_prev[...] + (1.0 - decay_rate) * total / all_rows
    cols_out[...] = new_cols
    by_col_out[...] = 1.0 / jnp.sqrt(new_cols)
    share = jnp.sum(both[1:2] / new_cols, axis=1, keepdims=True)
    total_out[...] = jnp.broadcast_to(share, total_out.shape)


def factors(elements, parts, by_row, by_col):
    total = parts[0][0:1, 0:1]
    for part in parts[1:]:
        total = total + part[0:1, 0:1]
    clip = jnp.maximum(1.0, jnp.sqrt(total / elements))
    return by_row[...] / clip, by_col[...]


def fresh_kernel(n, elements, low, high, weight, row_factor, col_factor, *refs):
    parts, outs = refs[:n], refs[n:]
    by_row, by_col = factors(elements, parts, row_factor, col_factor)
    n_chunks, chunk = by_row.shape
    split = outs[0].shape[0]
    for j in range(n_chunks):
        column = as_column(by_row[j : j + 1])
        first, last = j * chunk, (j + 1) * chunk
        for grads, here, there in columns_of((low, high)):
            update = grads[first:last, here] * column * by_col[:, there]
            fresh = (weight[first:last, there] - learn_rate * update).astype(jnp.bfloat16)
            if first < split:
                outs[0][first : min(last, split), there] = fresh[: min(last, split) - first]
            if last > split:
                cut = max(first, split)
                outs[1][cut - split : last - split, there] = fresh[cut - first :]


def update_kernel(n, elements, low, high, row_factor, col_factor, *refs):
    parts, out = refs[:n], refs[n]
    by_row, by_col = factors(elements, parts, row_factor, col_factor)
    n_chunks, chunk = by_row.shape
    for j in range(n_chunks):
        column = as_column(by_row[j : j + 1])
        for grads, here, there in columns_of((low, high)):
            at = slice(j * chunk, (j + 1) * chunk)
            out[at, there] = grads[at, here] * column * by_col[:, there]


def place_kernel(rows_of, *refs):
    pieces, out, sems = refs[: len(rows_of)], refs[-2], refs[-1]
    copies = []
    for k, piece in enumerate(pieces):
        at = pl.ds(pl.multiple_of(rows_of[k](), 16), piece.shape[0])
        copies.append(pltpu.make_async_copy(piece, out.at[at], sems.at[k]))
    for copy in copies:
        copy.start()
    for copy in copies:
        copy.wait()


FAR = pl.BlockSpec(memory_space=pltpu.HBM)
ANYWHERE = pl.BlockSpec(memory_space=pl.ANY)
NEAR = pl.BlockSpec(memory_space=pltpu.VMEM)


def call(kernel, out_shape, *args, flops=0, specs=None, moved=None, **more):
    outs = out_shape if isinstance(out_shape, (tuple, list)) else [out_shape]
    if moved is None:
        moved = sum(x.size * x.dtype.itemsize for x in [*args, *outs])
    return pl.pallas_call(
        kernel,
        out_shape=out_shape,
        in_specs=specs or [NEAR] * len(args),
        compiler_params=pltpu.CompilerParams(vmem_limit_bytes=VMEM_LIMIT),
        cost_estimate=pl.CostEstimate(flops=flops, bytes_accessed=moved, transcendentals=0),
        **more,
    )(*args)


def shape_of(*dims, dtype=jnp.float32):
    return jax.ShapeDtypeStruct(dims, dtype)


def fetch(hidden, grad_out, starts_of, rows):
    if rows % 128 or not starts_of:
        return cut(hidden, starts_of, rows), grad_out
    far = lambda x: pltpu.with_memory_space_constraint(x, pltpu.HBM)
    blocks = [shape_of(hidden.shape[0], rows, dtype=hidden.dtype)] * len(starts_of)
    *blocks, grad_held = call(
        functools.partial(fetch_kernel, starts_of),
        blocks + [shape_of(*grad_out.shape, dtype=grad_out.dtype)],
        far(hidden),
        far(grad_out),
        specs=[FAR, FAR],
        moved=4 * (len(starts_of) * hidden.shape[0] * rows + grad_out.size),
        scratch_shapes=[pltpu.SemaphoreType.DMA((len(starts_of) + 1,))],
    )
    return blocks, grad_held


def cut(hidden, starts_of, rows):
    if rows % 128 or not starts_of:
        return [lax.dynamic_slice_in_dim(hidden, f(), rows, axis=1) for f in starts_of]
    shapes = [shape_of(hidden.shape[0], rows, dtype=hidden.dtype)] * len(starts_of)
    moved = 4 * len(starts_of) * hidden.shape[0] * rows
    return call(functools.partial(cut_kernel, starts_of), shapes, hidden, moved=moved)


def product(held, start_of, rows, peers, gs, coded, bases=(), light=False):
    half = gs[0].shape[1] // 2
    shapes = [
        shape_of(rows + TAIL, half, dtype=jnp.bfloat16) if c else shape_of(rows, half) for c in coded
    ]
    placed = start_of is not None and rows % 128 == 0
    hs = list(peers)
    if placed:
        hs = [held] + hs
    elif start_of is not None:
        hs = [lax.dynamic_slice_in_dim(held, start_of(), rows, axis=1)] + hs
    flops = sum(2 * g.size * rows for g in gs)
    moved = sum(x.size * x.dtype.itemsize for x in [*gs, *bases, *shapes])
    if light:
        flops, moved = 0, 1
    return call(
        functools.partial(product_kernel, (placed, len(hs), len(bases)), start_of, coded),
        shapes,
        *hs,
        *gs,
        *bases,
        flops=flops,
        moved=moved,
    )


def relay(base, messages):
    rows, half = base.shape
    shape = shape_of(rows + TAIL, half, dtype=jnp.bfloat16)
    return call(functools.partial(relay_kernel, len(messages)), shape, base, *messages)


def gather(base, messages):
    if not messages:
        return base
    shape = shape_of(*base.shape)
    return call(functools.partial(gather_kernel, len(messages)), shape, base, *messages)


def final(base, messages, before=()):
    rows, half = base.shape
    chunk = chunk_of(rows)
    shapes = [shape_of(rows, half), shape_of(rows // chunk, chunk), shape_of(1, half)]
    kernel = functools.partial(final_kernel, len(messages), len(before))
    return call(kernel, shapes, base, *messages, *before)


def place(pieces, rows_of, out):
    n = len(pieces)
    old = [] if isinstance(out, jax.ShapeDtypeStruct) else [out]
    return call(
        functools.partial(place_kernel, rows_of),
        jax.ShapeDtypeStruct(out.shape, out.dtype),
        *pieces,
        *old,
        specs=[NEAR] * n + [ANYWHERE] * len(old),
        moved=sum(4 * p.size for p in pieces),
        out_specs=ANYWHERE,
        scratch_shapes=[pltpu.SemaphoreType.DMA((n,))],
        input_output_aliases={n: 0} if old else {},
    )


def after(x, *others):
    return lax.optimization_barrier((x, others))[0]


def grid_of(seq):
    hi = int(math.isqrt(seq))
    while seq % hi:
        hi -= 1
    return hi, seq // hi


def solution(mesh):
    n_dp, n_seq, n_tensor = (mesh.shape[name] for name in ("dp", "seq", "tensor"))
    n_hi, n_lo = grid_of(n_seq)
    his, los = range(1, n_hi), range(1, n_lo)

    def shift(x, hi=0, lo=0):
        pairs = [
            (a * n_lo + b, (a + hi) % n_hi * n_lo + (b + lo) % n_lo)
            for a in range(n_hi)
            for b in range(n_lo)
        ]
        return lax.ppermute(x, "seq", pairs)

    def turn(x, axis, n, step):
        return lax.ppermute(x, axis, [(a, (a + step) % n) for a in range(n)])

    def exchange(parts, axis, n, step=None):
        step = step or (lambda x, d: turn(x, axis, n, d))
        if axis is not None and n & (n - 1) == 0:
            d = 1
            while d < n:
                x = sum(parts[1:], parts[0])
                parts = [x, lax.ppermute(x, axis, [(a, a ^ d) for a in range(n)])]
                d *= 2
            return parts
        if n == 1:
            return parts
        x = sum(parts[1:], parts[0])
        return [x] + [step(x, d) for d in range(1, n)]

    def per_device(hidden, grad_out, master_weight, row_prev, col_prev):
        rows, cols = master_weight.shape

        part_rows = rows // 2
        all_rows, all_cols = rows * n_dp * n_seq, cols * n_tensor

        def block_of(hi, lo):
            seq = lax.axis_index("seq")
            mine = lax.div(seq, n_lo), lax.rem(seq, n_lo)
            return lax.rem(mine[0] + hi, n_hi) * n_lo + lax.rem(mine[1] + lo, n_lo)

        def start_of(p, hi, lo):
            return lambda: (
                lax.rem(lax.axis_index("dp") + p, n_dp) * n_seq + block_of(hi, lo)
            ) * rows

        def row_of(part, hi, lo):
            return lambda: block_of(n_hi - hi, n_lo - lo) * rows + part * part_rows

        gs = [turn(grad_out, "dp", n_dp, p) for p in range(1, n_dp)]
        far_group = [(hi, lo) for hi in his for lo in los]
        near_group = [(0, lo) for lo in los] + [(hi, 0) for hi in his] + [(0, 0)]
        blocks = {at: [] for at in far_group + near_group}
        for group in (far_group, near_group):
            keys = [(p, at) for at in group for p in range(1, n_dp)]
            starts = [start_of(p, *at) for p, at in keys]
            if group is far_group:
                sent, grad_out = fetch(hidden, grad_out, starts, rows)
            else:
                sent = cut(hidden, starts, rows)
            for (p, at), block in zip(keys, sent):
                blocks[at].append(turn(block, "dp", n_dp, p))
        gs = [grad_out] + gs

        far = [{}, {}]
        for hi, lo in far_group:
            bases = product(hidden, start_of(0, hi, lo), rows, [], gs[:1], (False, False))
            if n_dp > 1:
                coded = product(None, None, rows, blocks[hi, lo], gs[1:], (True, True), bases)
            else:
                coded = [relay(x, []) for x in bases]
            far[0][hi, lo] = shift(coded[0], lo=lo)
            far[1][hi, lo] = shift(coded[1], hi=hi)

        def whole_product(hi, lo, coded):
            peers = blocks[hi, lo]
            return product(hidden, start_of(0, hi, lo), rows, peers, gs, coded, light=True)

        near, base = [{}, {}], [{}, {}]
        for lo in los:
            first, base[1][lo] = whole_product(0, lo, (True, False))
            near[0][lo] = shift(first, lo=lo)
        for hi in his:
            base[0][hi], second = whole_product(hi, 0, (False, True))
            near[1][hi] = shift(second, hi=hi)
        own = whole_product(0, 0, (False, False))
        last = [{}, {}]
        for hi in his:
            message = relay(base[0][hi], [far[0][hi, lo] for lo in los])
            last[0][hi] = shift(message, hi=hi)
        for lo in los:
            message = relay(base[1][lo], [far[1][hi, lo] for hi in his])
            last[1][lo] = shift(message, lo=lo)
        own = [gather(own[part], list(near[part].values())) for part in (0, 1)]
        low, row_part, low_col = final(own[0], list(last[0].values()))
        high, row_part, high_col = final(own[1], list(last[1].values()), [row_part])

        chunks = row_part.shape
        parts = exchange([row_part], "tensor", n_tensor)
        new_rows, by_row, both = call(
            functools.partial(rows_kernel, len(parts), all_cols),
            [shape_of(*chunks), shape_of(*chunks), shape_of(2, cols)],
            low,
            high,
            row_prev.reshape(chunks),
            low_col,
            high_col,
            *parts,
        )
        parts = exchange([both], "dp", n_dp)
        x = sum(parts[1:], parts[0])
        if n_hi * n_lo <= 4:
            steps = [(hi, lo) for hi in range(n_hi) for lo in range(n_lo) if hi or lo]
            parts = [x] + [shift(x, hi=hi, lo=lo) for hi, lo in steps]
        else:
            parts = exchange([x], None, n_lo, lambda x, d: shift(x, lo=d))
            parts = exchange(parts, None, n_hi, lambda x, d: shift(x, hi=d))
        new_cols, by_col, share = call(
            functools.partial(cols_kernel, len(parts), all_rows),
            [shape_of(1, cols), shape_of(1, cols), shape_of(1, 128)],
            col_prev.reshape(1, cols),
            *parts,
        )
        parts = exchange([share], "tensor", n_tensor)
        elements = all_rows * all_cols

        pair = call(
            functools.partial(fresh_kernel, len(parts), elements),
            [shape_of(part_rows, cols, dtype=jnp.bfloat16)] * 2,
            low,
            high,
            master_weight,
            by_row,
            by_col,
            *parts,
        )
        along_lo, along_hi = {}, {}
        for lo in los:
            along_lo[0, lo] = shift(pair[0], lo=lo)
        for hi in his:
            along_hi[1, hi] = shift(pair[1], hi=hi)
        for lo in los:
            along_lo[1, lo] = shift(pair[1], lo=lo)
        for hi in his:
            along_hi[0, hi] = shift(pair[0], hi=hi)

        onward = []
        for hi in his:
            for lo in los:
                onward.append((shift(along_lo[0, lo], hi=hi), row_of(0, hi, lo)))
                onward.append((shift(along_hi[1, hi], lo=lo), row_of(1, hi, lo)))
        update = call(
            functools.partial(update_kernel, len(parts), elements),
            shape_of(rows, cols),
            after(low, *along_lo.values()),
            high,
            by_row,
            by_col,
            *parts,
        )

        whole = jax.ShapeDtypeStruct((rows * n_seq, cols), jnp.bfloat16)
        new_weight = place(pair, [row_of(part, 0, 0) for part in (0, 1)], whole)
        pieces = [(x, row_of(part, 0, lo)) for (part, lo), x in along_lo.items()]
        pieces += [(x, row_of(part, hi, 0)) for (part, hi), x in along_hi.items()]
        for group in [pieces, onward]:
            if group:
                new_weight = place([x for x, _ in group], [f for _, f in group], new_weight)
        return (new_weight, update, new_rows.reshape(rows), new_cols.reshape(cols))

    return jax.shard_map(
        per_device,
        mesh=mesh,
        in_specs=(
            P(("dp", "seq"), None),
            P(("dp", "seq"), "tensor"),
            P(("dp", "seq"), "tensor"),
            P(("dp", "seq")),
            P("tensor"),
        ),
        out_specs=(P("dp", "tensor"), P(("dp", "seq"), "tensor"), P(("dp", "seq")), P("tensor")),
        check_vma=False,
    )
```

```python
import functools
import math

import jax
import jax.numpy as jnp
from jax import lax
from jax.experimental import pallas as pl
from jax.experimental.pallas import tpu as pltpu
from jax.sharding import PartitionSpec as P

decay_rate = 0.8
learn_rate = 0.05
small_term = 1e-06

POWER = 11
TOP = 2.0 ** (125.0 / POWER)
TAIL = 16
VMEM_LIMIT = 16 * 2**20


def chunk_of(rows):
    return 128 if rows % 128 == 0 else rows


def groups_of(rows):
    n = rows // chunk_of(rows)
    cuts = sorted({0, (n + 1) // 2, n})
    return [(a * chunk_of(rows), b * chunk_of(rows)) for a, b in zip(cuts, cuts[1:])]


def encode(x):
    top = jnp.max(jnp.abs(x), axis=0, keepdims=True)
    scale = jnp.maximum(top * 1.004, 1e-30).astype(jnp.bfloat16).astype(jnp.float32)
    u = x * (TOP / scale)
    u2 = u * u
    u4 = u2 * u2
    return (u4 * u4 * u2 * u).astype(jnp.bfloat16), scale


def decode(code, scale):
    code = code.astype(jnp.float32)
    size = jnp.abs(code)
    u = jnp.exp(jnp.log(jnp.maximum(size, 1e-37)) * (1.0 / POWER)) * (scale * (1.0 / TOP))
    return jnp.where(size > 1e-37, jnp.where(code > 0, u, -u), 0.0)


def write_scales(ref, scales):
    rows, cols = ref.shape
    at = lax.broadcasted_iota(jnp.int32, (TAIL, cols), 0)
    tail = jnp.zeros((TAIL, cols), jnp.float32)
    for j, scale in enumerate(scales):
        tail = jnp.where(at == j, scale, tail)
    ref[rows - TAIL :] = tail.astype(jnp.bfloat16)


def read_scales(ref):
    return ref[ref.shape[0] - TAIL :].astype(jnp.float32)


def product_kernel(layout, start_of, coded, *refs):
    placed, n_hs, n_base = layout
    refs = list(refs)
    take = lambda k: [refs.pop(0) for _ in range(k)]
    hs, gs, bases, outs = take(n_hs), take(n_hs), take(n_base), refs
    cols = gs[0].shape[1]
    rows = outs[0].shape[0] - (TAIL if coded[0] else 0)
    half, chunk = cols // 2, chunk_of(rows)
    first = [start_of() if k == 0 and placed else 0 for k in range(n_hs)]
    scales = [[], []]
    for j in range(rows // chunk):
        at = slice(j * chunk, (j + 1) * chunk)
        total = None
        for k, (h, g) in enumerate(zip(hs, gs)):
            if k == 0 and placed:
                block = h[:, pl.ds(pl.multiple_of(first[k] + j * chunk, chunk), chunk)]
            else:
                block = h[:, at]
            term = lax.dot_general(
                block, g[...], (((0,), (0,)), ((), ())), preferred_element_type=jnp.float32
            )
            total = term if total is None else total + term
        for part in (0, 1):
            x = total[:, part * half : (part + 1) * half]
            if bases:
                x = x + bases[part][at]
            if coded[part]:
                outs[part][at], scale = encode(x)
                scales[part].append(scale)
            else:
                outs[part][at] = x
    for part in (0, 1):
        if coded[part]:
            write_scales(outs[part], scales[part])


def fetch_kernel(starts_of, hidden, grad_out, *refs):
    outs, grad_held, sems = refs[:-2], refs[-2], refs[-1]
    copies = []
    for k, (start_of, out) in enumerate(zip(starts_of, outs)):
        at = pl.ds(pl.multiple_of(start_of(), 128), out.shape[1])
        copies.append(pltpu.make_async_copy(hidden.at[:, at], out, sems.at[k]))
        copies[k].start()
    copies.append(pltpu.make_async_copy(grad_out, grad_held, sems.at[len(outs)]))
    copies[-1].start()
    for copy in copies:
        copy.wait()


def cut_kernel(starts_of, hidden, *outs):
    for start_of, out in zip(starts_of, outs):
        out[...] = hidden[:, pl.ds(pl.multiple_of(start_of(), 128), out.shape[1])]


def added_up(base, messages, group, begin):
    chunk = chunk_of(base.shape[0])
    tails = [read_scales(m) for m in messages]
    for row in range(*group, chunk):
        total = base[row : row + chunk]
        j = (row - begin) // chunk
        for m, tail in zip(messages, tails):
            total = total + decode(m[row - begin : row - begin + chunk], tail[j : j + 1])
        yield slice(row, row + chunk), total


def relay_kernel(n, group, base, *refs):
    messages, out = refs[:n], refs[n]
    scales = []
    for at, total in added_up(base, messages, group, 0):
        out[at.start - group[0] : at.stop - group[0]], scale = encode(total)
        scales.append(scale)
    write_scales(out, scales)


def gather_kernel(base, *refs):
    messages, out = refs[:-1], refs[-1]
    for at, total in added_up(base, messages, (0, base.shape[0]), 0):
        out[at] = total


def final_kernel(n, group, has_rows, has_cols, base, *refs):
    refs = list(refs)
    messages = [refs.pop(0) for _ in range(n)]
    rows_in = refs.pop(0)[...] if has_rows else None
    cols_in = refs.pop(0)[...] if has_cols else 0.0
    out, row_out, col_out = refs
    chunk, half = chunk_of(base.shape[0]), base.shape[1]
    row_out[...] = rows_in if has_rows else jnp.zeros(row_out.shape, jnp.float32)
    col_sum = jnp.zeros((1, half), jnp.float32) + cols_in
    for at, total in added_up(base, messages, group, group[0]):
        out[at.start - group[0] : at.stop - group[0]] = total
        squares = total * total
        col_sum = col_sum + jnp.sum(squares, axis=0, keepdims=True)
        row_sum = jnp.zeros((chunk, 128), jnp.float32)
        for k in range(half // 128):
            row_sum = row_sum + squares[:, k * 128 : (k + 1) * 128]
        row_sum = jnp.sum(row_sum.T, axis=0, keepdims=True)
        j = at.start // chunk
        row_out[j : j + 1] = row_sum + (rows_in[j : j + 1] if has_rows else 0.0)
    col_out[...] = col_sum


def tiles_of(pieces, first, last):
    half, begin = pieces[0].shape[1], 0
    for low, high in zip(pieces[::2], pieces[1::2]):
        end = begin + low.shape[0]
        if begin <= first < end:
            for part, ref in enumerate((low, high)):
                for k in range(0, half, 128):
                    tile = ref[first - begin : last - begin, k : k + 128]
                    yield tile, slice(part * half + k, part * half + k + 128)
        begin = end


def as_column(row):
    return jnp.broadcast_to(row, (128, row.shape[1])).T


def tree_sum(terms):
    while len(terms) > 1:
        pairs = [sum(terms[k + 1 : k + 2], terms[k]) for k in range(0, len(terms), 2)]
        terms = pairs
    return terms[0]


def rows_kernel(n, n_pieces, all_cols, *refs):
    pieces, refs = refs[:n_pieces], refs[n_pieces:]
    (row_prev, low_col, high_col), refs = refs[:3], refs[3:]
    parts, (rows_out, by_row_out, both_out) = refs[:n], refs[n:]
    total = tree_sum([p[...] for p in parts])
    total = total + small_term * all_cols
    new_rows = decay_rate * row_prev[...] + (1.0 - decay_rate) * total / all_cols
    rows_out[...] = new_rows
    by_row_out[...] = 1.0 / jnp.sqrt(new_rows)
    inverse = 1.0 / new_rows
    n_chunks, chunk = new_rows.shape
    half = low_col.shape[1]
    sums = [jnp.zeros((1, 128), jnp.float32)] * (2 * half // 128)
    for j in range(n_chunks):
        weight = as_column(inverse[j : j + 1])
        for k, (g, _) in enumerate(tiles_of(pieces, j * chunk, (j + 1) * chunk)):
            sums[k] = sums[k] + jnp.sum(g * g * weight, axis=0, keepdims=True)
    both_out[0:1, :half] = low_col[...]
    both_out[0:1, half:] = high_col[...]
    for k, total in enumerate(sums):
        both_out[1:2, k * 128 : (k + 1) * 128] = total


def cols_kernel(n, all_rows, col_prev, *refs):
    parts, (cols_out, by_col_out, total_out) = refs[:n], refs[n:]
    both = tree_sum([p[...] for p in parts])
    total = both[0:1] + small_term * all_rows
    new_cols = decay_rate * col_prev[...] + (1.0 - decay_rate) * total / all_rows
    cols_out[...] = new_cols
    by_col_out[...] = 1.0 / jnp.sqrt(new_cols)
    share = jnp.sum(both[1:2] / new_cols, axis=1, keepdims=True)
    total_out[...] = jnp.broadcast_to(share, total_out.shape)


def factors(elements, parts, by_row, by_col):
    total = parts[0][0:1, 0:1]
    for part in parts[1:]:
        total = total + part[0:1, 0:1]
    clip = jnp.maximum(1.0, jnp.sqrt(total / elements))
    return by_row[...] / clip, by_col[...]


def fresh_kernel(n, n_pieces, elements, *refs):
    pieces, refs = refs[:n_pieces], refs[n_pieces:]
    (weight, row_factor, col_factor), refs = refs[:3], refs[3:]
    parts, outs = refs[:n], refs[n:]
    by_row, by_col = factors(elements, parts, row_factor, col_factor)
    n_chunks, chunk = by_row.shape
    split = outs[0].shape[0]
    for j in range(n_chunks):
        column = as_column(by_row[j : j + 1])
        first, last = j * chunk, (j + 1) * chunk
        for grads, there in tiles_of(pieces, first, last):
            update = grads * column * by_col[:, there]
            fresh = (weight[first:last, there] - learn_rate * update).astype(jnp.bfloat16)
            if first < split:
                outs[0][first : min(last, split), there] = fresh[: min(last, split) - first]
            if last > split:
                cut = max(first, split)
                outs[1][cut - split : last - split, there] = fresh[cut - first :]


def update_kernel(n, n_pieces, elements, *refs):
    pieces, refs = refs[:n_pieces], refs[n_pieces:]
    (row_factor, col_factor), refs = refs[:2], refs[2:]
    parts, out = refs[:n], refs[n]
    by_row, by_col = factors(elements, parts, row_factor, col_factor)
    n_chunks, chunk = by_row.shape
    for j in range(n_chunks):
        column = as_column(by_row[j : j + 1])
        first, last = j * chunk, (j + 1) * chunk
        for grads, there in tiles_of(pieces, first, last):
            out[first:last, there] = grads * column * by_col[:, there]


def place_kernel(rows_of, *refs):
    pieces, out, sems = refs[: len(rows_of)], refs[-2], refs[-1]
    copies = []
    for k, piece in enumerate(pieces):
        at = pl.ds(pl.multiple_of(rows_of[k](), 16), piece.shape[0])
        copies.append(pltpu.make_async_copy(piece, out.at[at], sems.at[k]))
    for copy in copies:
        copy.start()
    for copy in copies:
        copy.wait()


FAR = pl.BlockSpec(memory_space=pltpu.HBM)
ANYWHERE = pl.BlockSpec(memory_space=pl.ANY)
NEAR = pl.BlockSpec(memory_space=pltpu.VMEM)


def call(kernel, out_shape, *args, flops=0, specs=None, moved=None, **more):
    outs = out_shape if isinstance(out_shape, (tuple, list)) else [out_shape]
    if moved is None:
        moved = sum(x.size * x.dtype.itemsize for x in [*args, *outs])
    return pl.pallas_call(
        kernel,
        out_shape=out_shape,
        in_specs=specs or [NEAR] * len(args),
        compiler_params=pltpu.CompilerParams(vmem_limit_bytes=VMEM_LIMIT),
        cost_estimate=pl.CostEstimate(flops=flops, bytes_accessed=moved, transcendentals=0),
        **more,
    )(*args)


def shape_of(*dims, dtype=jnp.float32):
    return jax.ShapeDtypeStruct(dims, dtype)


def fetch(hidden, grad_out, starts_of, rows):
    if rows % 128 or not starts_of:
        return cut(hidden, starts_of, rows), grad_out
    far = lambda x: pltpu.with_memory_space_constraint(x, pltpu.HBM)
    blocks = [shape_of(hidden.shape[0], rows, dtype=hidden.dtype)] * len(starts_of)
    *blocks, grad_held = call(
        functools.partial(fetch_kernel, starts_of),
        blocks + [shape_of(*grad_out.shape, dtype=grad_out.dtype)],
        far(hidden),
        far(grad_out),
        specs=[FAR, FAR],
        moved=4 * (len(starts_of) * hidden.shape[0] * rows + grad_out.size),
        scratch_shapes=[pltpu.SemaphoreType.DMA((len(starts_of) + 1,))],
    )
    return blocks, grad_held


def cut(hidden, starts_of, rows):
    if rows % 128 or not starts_of:
        return [lax.dynamic_slice_in_dim(hidden, f(), rows, axis=1) for f in starts_of]
    shapes = [shape_of(hidden.shape[0], rows, dtype=hidden.dtype)] * len(starts_of)
    moved = 4 * len(starts_of) * hidden.shape[0] * rows
    return call(functools.partial(cut_kernel, starts_of), shapes, hidden, moved=moved)


def product(held, start_of, rows, peers, gs, coded, bases=(), light=False):
    half = gs[0].shape[1] // 2
    shapes = [
        shape_of(rows + TAIL, half, dtype=jnp.bfloat16) if c else shape_of(rows, half) for c in coded
    ]
    placed = start_of is not None and rows % 128 == 0
    hs = list(peers)
    if placed:
        hs = [held] + hs
    elif start_of is not None:
        hs = [lax.dynamic_slice_in_dim(held, start_of(), rows, axis=1)] + hs
    flops = sum(2 * g.size * rows for g in gs)
    moved = sum(x.size * x.dtype.itemsize for x in [*gs, *bases, *shapes])
    if light:
        flops, moved = 0, 1
    return call(
        functools.partial(product_kernel, (placed, len(hs), len(bases)), start_of, coded),
        shapes,
        *hs,
        *gs,
        *bases,
        flops=flops,
        moved=moved,
    )


def relay(base, messages, group):
    shape = shape_of(group[1] - group[0] + TAIL, base.shape[1], dtype=jnp.bfloat16)
    return call(functools.partial(relay_kernel, len(messages), group), shape, base, *messages)


def gather(base, messages):
    if not messages:
        return base
    return call(gather_kernel, shape_of(*base.shape), base, *messages)


def final(base, messages, group, rows_in, cols_in):
    rows, half = base.shape
    chunk = chunk_of(rows)
    shapes = [
        shape_of(group[1] - group[0], half),
        shape_of(rows // chunk, chunk),
        shape_of(1, half),
    ]
    kernel = functools.partial(
        final_kernel, len(messages), group, rows_in is not None, cols_in is not None
    )
    more = [x for x in (rows_in, cols_in) if x is not None]
    return call(kernel, shapes, base, *messages, *more)


def place(pieces, rows_of, out):
    n = len(pieces)
    old = [] if isinstance(out, jax.ShapeDtypeStruct) else [out]
    return call(
        functools.partial(place_kernel, rows_of),
        jax.ShapeDtypeStruct(out.shape, out.dtype),
        *pieces,
        *old,
        specs=[NEAR] * n + [ANYWHERE] * len(old),
        moved=sum(4 * p.size for p in pieces),
        out_specs=ANYWHERE,
        scratch_shapes=[pltpu.SemaphoreType.DMA((n,))],
        input_output_aliases={n: 0} if old else {},
    )


def after(x, *others):
    return lax.optimization_barrier((x, others))[0]


def grid_of(seq):
    hi = int(math.isqrt(seq))
    while seq % hi:
        hi -= 1
    return hi, seq // hi


def solution(mesh):
    n_dp, n_seq, n_tensor = (mesh.shape[name] for name in ("dp", "seq", "tensor"))
    n_hi, n_lo = grid_of(n_seq)
    his, los = range(1, n_hi), range(1, n_lo)

    def shift(x, hi=0, lo=0):
        pairs = [
            (a * n_lo + b, (a + hi) % n_hi * n_lo + (b + lo) % n_lo)
            for a in range(n_hi)
            for b in range(n_lo)
        ]
        return lax.ppermute(x, "seq", pairs)

    def turn(x, axis, n, step):
        return lax.ppermute(x, axis, [(a, (a + step) % n) for a in range(n)])

    def exchange(parts, axis, n, step=None):
        step = step or (lambda x, d: turn(x, axis, n, d))
        if axis is not None and n & (n - 1) == 0:
            d = 1
            while d < n:
                x = sum(parts[1:], parts[0])
                parts = [x, lax.ppermute(x, axis, [(a, a ^ d) for a in range(n)])]
                d *= 2
            return parts
        if n == 1:
            return parts
        x = sum(parts[1:], parts[0])
        return [x] + [step(x, d) for d in range(1, n)]

    def per_device(hidden, grad_out, master_weight, row_prev, col_prev):
        rows, cols = master_weight.shape

        part_rows = rows // 2
        all_rows, all_cols = rows * n_dp * n_seq, cols * n_tensor

        def block_of(hi, lo):
            seq = lax.axis_index("seq")
            mine = lax.div(seq, n_lo), lax.rem(seq, n_lo)
            return lax.rem(mine[0] + hi, n_hi) * n_lo + lax.rem(mine[1] + lo, n_lo)

        def start_of(p, hi, lo):
            return lambda: (
                lax.rem(lax.axis_index("dp") + p, n_dp) * n_seq + block_of(hi, lo)
            ) * rows

        def row_of(part, hi, lo):
            return lambda: block_of(n_hi - hi, n_lo - lo) * rows + part * part_rows

        gs = [turn(grad_out, "dp", n_dp, p) for p in range(1, n_dp)]
        far_group = [(hi, lo) for hi in his for lo in los]
        near_group = [(0, lo) for lo in los] + [(hi, 0) for hi in his] + [(0, 0)]
        blocks = {at: [] for at in far_group + near_group}
        for group in (far_group, near_group):
            keys = [(p, at) for at in group for p in range(1, n_dp)]
            starts = [start_of(p, *at) for p, at in keys]
            if group is far_group:
                sent, grad_out = fetch(hidden, grad_out, starts, rows)
            else:
                sent = cut(hidden, starts, rows)
            for (p, at), block in zip(keys, sent):
                blocks[at].append(turn(block, "dp", n_dp, p))
        gs = [grad_out] + gs

        far = [{}, {}]
        for hi, lo in far_group:
            bases = product(hidden, start_of(0, hi, lo), rows, [], gs[:1], (False, False))
            if n_dp > 1:
                coded = product(None, None, rows, blocks[hi, lo], gs[1:], (True, True), bases)
            else:
                coded = [relay(x, [], (0, rows)) for x in bases]
            far[0][hi, lo] = shift(coded[0], lo=lo)
            far[1][hi, lo] = shift(coded[1], hi=hi)

        def whole_product(hi, lo, coded):
            peers = blocks[hi, lo]
            return product(hidden, start_of(0, hi, lo), rows, peers, gs, coded, light=True)

        near, base = [{}, {}], [{}, {}]
        for lo in los:
            first, base[1][lo] = whole_product(0, lo, (True, False))
            near[0][lo] = shift(first, lo=lo)
        for hi in his:
            base[0][hi], second = whole_product(hi, 0, (False, True))
            near[1][hi] = shift(second, hi=hi)
        own = whole_product(0, 0, (False, False))
        groups = groups_of(rows)
        last = [{}, {}]
        for group in groups:
            for hi in his:
                message = relay(base[0][hi], [far[0][hi, lo] for lo in los], group)
                last[0].setdefault(group, []).append(shift(message, hi=hi))
            for lo in los:
                message = relay(base[1][lo], [far[1][hi, lo] for hi in his], group)
                last[1].setdefault(group, []).append(shift(message, lo=lo))
        own = [gather(own[part], list(near[part].values())) for part in (0, 1)]
        grads, row_part, col_part = [], None, [None, None]
        for group in groups:
            for part in (0, 1):
                messages = last[part].get(group, [])
                piece, row_part, col_part[part] = final(
                    own[part], messages, group, row_part, col_part[part]
                )
                grads.append(piece)

        chunks = row_part.shape
        parts = exchange([row_part], "tensor", n_tensor)
        new_rows, by_row, both = call(
            functools.partial(rows_kernel, len(parts), len(grads), all_cols),
            [shape_of(*chunks), shape_of(*chunks), shape_of(2, cols)],
            *grads,
            row_prev.reshape(chunks),
            *col_part,
            *parts,
        )
        parts = exchange([both], "dp", n_dp)
        x = sum(parts[1:], parts[0])
        if n_hi * n_lo <= 4:
            steps = [(hi, lo) for hi in range(n_hi) for lo in range(n_lo) if hi or lo]
            parts = [x] + [shift(x, hi=hi, lo=lo) for hi, lo in steps]
        else:
            parts = exchange([x], None, n_lo, lambda x, d: shift(x, lo=d))
            parts = exchange(parts, None, n_hi, lambda x, d: shift(x, hi=d))
        new_cols, by_col, share = call(
            functools.partial(cols_kernel, len(parts), all_rows),
            [shape_of(1, cols), shape_of(1, cols), shape_of(1, 128)],
            col_prev.reshape(1, cols),
            *parts,
        )
        parts = exchange([share], "tensor", n_tensor)
        elements = all_rows * all_cols

        pair = call(
            functools.partial(fresh_kernel, len(parts), len(grads), elements),
            [shape_of(part_rows, cols, dtype=jnp.bfloat16)] * 2,
            *grads,
            master_weight,
            by_row,
            by_col,
            *parts,
        )
        along_lo, along_hi = {}, {}
        for lo in los:
            along_lo[0, lo] = shift(pair[0], lo=lo)
        for hi in his:
            along_hi[1, hi] = shift(pair[1], hi=hi)
        for lo in los:
            along_lo[1, lo] = shift(pair[1], lo=lo)
        for hi in his:
            along_hi[0, hi] = shift(pair[0], hi=hi)

        onward = []
        for hi in his:
            for lo in los:
                onward.append((shift(along_lo[0, lo], hi=hi), row_of(0, hi, lo)))
                onward.append((shift(along_hi[1, hi], lo=lo), row_of(1, hi, lo)))
        update = call(
            functools.partial(update_kernel, len(parts), len(grads), elements),
            shape_of(rows, cols),
            after(grads[0], *along_lo.values()),
            *grads[1:],
            by_row,
            by_col,
            *parts,
        )

        whole = jax.ShapeDtypeStruct((rows * n_seq, cols), jnp.bfloat16)
        new_weight = place(pair, [row_of(part, 0, 0) for part in (0, 1)], whole)
        pieces = [(x, row_of(part, 0, lo)) for (part, lo), x in along_lo.items()]
        pieces += [(x, row_of(part, hi, 0)) for (part, hi), x in along_hi.items()]
        for group in [pieces, onward]:
            if group:
                new_weight = place([x for x, _ in group], [f for _, f in group], new_weight)
        return (new_weight, update, new_rows.reshape(rows), new_cols.reshape(cols))

    return jax.shard_map(
        per_device,
        mesh=mesh,
        in_specs=(
            P(("dp", "seq"), None),
            P(("dp", "seq"), "tensor"),
            P(("dp", "seq"), "tensor"),
            P(("dp", "seq")),
            P("tensor"),
        ),
        out_specs=(P("dp", "tensor"), P(("dp", "seq"), "tensor"), P(("dp", "seq")), P("tensor")),
        check_vma=False,
    )
```

```python
import functools
import math

import jax
import jax.numpy as jnp
from jax import lax
from jax.experimental import pallas as pl
from jax.experimental.pallas import tpu as pltpu
from jax.sharding import PartitionSpec as P

decay_rate = 0.8
learn_rate = 0.05
small_term = 1e-06

POWER = 11
TOP = 2.0 ** (125.0 / POWER)
TAIL = 16
VMEM_LIMIT = 16 * 2**20


def chunk_of(rows):
    return 128 if rows % 128 == 0 else rows


def groups_of(rows):
    n = rows // chunk_of(rows)
    cuts = sorted({0, (n + 1) // 2, n})
    return [(a * chunk_of(rows), b * chunk_of(rows)) for a, b in zip(cuts, cuts[1:])]


def encode(x):
    top = jnp.max(jnp.abs(x), axis=0, keepdims=True)
    scale = jnp.maximum(top * 1.004, 1e-30).astype(jnp.bfloat16).astype(jnp.float32)
    u = x * (TOP / scale)
    u2 = u * u
    u4 = u2 * u2
    return (u4 * u4 * u2 * u).astype(jnp.bfloat16), scale


def decode(code, scale):
    code = code.astype(jnp.float32)
    size = jnp.abs(code)
    u = jnp.exp(jnp.log(jnp.maximum(size, 1e-37)) * (1.0 / POWER)) * (scale * (1.0 / TOP))
    return jnp.where(size > 1e-37, jnp.where(code > 0, u, -u), 0.0)


def write_scales(ref, scales):
    rows, cols = ref.shape
    at = lax.broadcasted_iota(jnp.int32, (TAIL, cols), 0)
    tail = jnp.zeros((TAIL, cols), jnp.float32)
    for j, scale in enumerate(scales):
        tail = jnp.where(at == j, scale, tail)
    ref[rows - TAIL :] = tail.astype(jnp.bfloat16)


def read_scales(ref):
    return ref[ref.shape[0] - TAIL :].astype(jnp.float32)


def product_kernel(layout, start_of, coded, *refs):
    placed, n_hs, n_base = layout
    refs = list(refs)
    take = lambda k: [refs.pop(0) for _ in range(k)]
    hs, gs, bases, outs = take(n_hs), take(n_hs), take(n_base), refs
    cols = gs[0].shape[1]
    rows = outs[0].shape[0] - (TAIL if coded[0] else 0)
    half, chunk = cols // 2, chunk_of(rows)
    first = [start_of() if k == 0 and placed else 0 for k in range(n_hs)]
    scales = [[], []]
    for j in range(rows // chunk):
        at = slice(j * chunk, (j + 1) * chunk)
        total = None
        for k, (h, g) in enumerate(zip(hs, gs)):
            if k == 0 and placed:
                block = h[:, pl.ds(pl.multiple_of(first[k] + j * chunk, chunk), chunk)]
            else:
                block = h[:, at]
            term = lax.dot_general(
                block, g[...], (((0,), (0,)), ((), ())), preferred_element_type=jnp.float32
            )
            total = term if total is None else total + term
        for part in (0, 1):
            x = total[:, part * half : (part + 1) * half]
            if bases:
                x = x + bases[part][at]
            if coded[part]:
                outs[part][at], scale = encode(x)
                scales[part].append(scale)
            else:
                outs[part][at] = x
    for part in (0, 1):
        if coded[part]:
            write_scales(outs[part], scales[part])


def fetch_kernel(starts_of, hidden, grad_out, *refs):
    outs, grad_held, sems = refs[:-2], refs[-2], refs[-1]
    copies = []
    for k, (start_of, out) in enumerate(zip(starts_of, outs)):
        at = pl.ds(pl.multiple_of(start_of(), 128), out.shape[1])
        copies.append(pltpu.make_async_copy(hidden.at[:, at], out, sems.at[k]))
        copies[k].start()
    copies.append(pltpu.make_async_copy(grad_out, grad_held, sems.at[len(outs)]))
    copies[-1].start()
    for copy in copies:
        copy.wait()


def cut_kernel(starts_of, hidden, *outs):
    for start_of, out in zip(starts_of, outs):
        out[...] = hidden[:, pl.ds(pl.multiple_of(start_of(), 128), out.shape[1])]


def added_up(base, messages, group, begin):
    chunk = chunk_of(base.shape[0])
    tails = [read_scales(m) for m in messages]
    for row in range(*group, chunk):
        total = base[row : row + chunk]
        j = (row - begin) // chunk
        for m, tail in zip(messages, tails):
            total = total + decode(m[row - begin : row - begin + chunk], tail[j : j + 1])
        yield slice(row, row + chunk), total


def relay_kernel(n, group, base, *refs):
    messages, out = refs[:n], refs[n]
    scales = []
    for at, total in added_up(base, messages, group, 0):
        out[at.start - group[0] : at.stop - group[0]], scale = encode(total)
        scales.append(scale)
    write_scales(out, scales)


def gather_kernel(base, *refs):
    messages, out = refs[:-1], refs[-1]
    for at, total in added_up(base, messages, (0, base.shape[0]), 0):
        out[at] = total


def final_kernel(n, group, has_rows, has_cols, base, *refs):
    refs = list(refs)
    messages = [refs.pop(0) for _ in range(n)]
    rows_in = refs.pop(0)[...] if has_rows else None
    cols_in = refs.pop(0)[...] if has_cols else 0.0
    out, row_out, col_out = refs
    chunk, half = chunk_of(base.shape[0]), base.shape[1]
    row_out[...] = rows_in if has_rows else jnp.zeros(row_out.shape, jnp.float32)
    col_sum = jnp.zeros((1, half), jnp.float32) + cols_in
    for at, total in added_up(base, messages, group, group[0]):
        out[at.start - group[0] : at.stop - group[0]] = total
        squares = total * total
        col_sum = col_sum + jnp.sum(squares, axis=0, keepdims=True)
        row_sum = jnp.zeros((chunk, 128), jnp.float32)
        for k in range(half // 128):
            row_sum = row_sum + squares[:, k * 128 : (k + 1) * 128]
        row_sum = jnp.sum(row_sum.T, axis=0, keepdims=True)
        j = at.start // chunk
        row_out[j : j + 1] = row_sum + (rows_in[j : j + 1] if has_rows else 0.0)
    col_out[...] = col_sum


def tiles_of(pieces, first, last):
    half, begin = pieces[0].shape[1], 0
    for low, high in zip(pieces[::2], pieces[1::2]):
        end = begin + low.shape[0]
        if begin <= first < end:
            for part, ref in enumerate((low, high)):
                for k in range(0, half, 128):
                    tile = ref[first - begin : last - begin, k : k + 128]
                    yield tile, slice(part * half + k, part * half + k + 128)
        begin = end


def as_column(row):
    return jnp.broadcast_to(row, (128, row.shape[1])).T


def tree_sum(terms):
    while len(terms) > 1:
        pairs = [sum(terms[k + 1 : k + 2], terms[k]) for k in range(0, len(terms), 2)]
        terms = pairs
    return terms[0]


def rows_kernel(n, n_pieces, all_cols, *refs):
    pieces, refs = refs[:n_pieces], refs[n_pieces:]
    (row_prev, low_col, high_col), refs = refs[:3], refs[3:]
    parts, (rows_out, by_row_out, both_out) = refs[:n], refs[n:]
    total = tree_sum([p[...] for p in parts])
    total = total + small_term * all_cols
    new_rows = decay_rate * row_prev[...] + (1.0 - decay_rate) * total / all_cols
    rows_out[...] = new_rows
    by_row_out[...] = 1.0 / jnp.sqrt(new_rows)
    inverse = 1.0 / new_rows
    n_chunks, chunk = new_rows.shape
    half = low_col.shape[1]
    sums = [jnp.zeros((1, 128), jnp.float32)] * (2 * half // 128)
    for j in range(n_chunks):
        weight = as_column(inverse[j : j + 1])
        for k, (g, _) in enumerate(tiles_of(pieces, j * chunk, (j + 1) * chunk)):
            sums[k] = sums[k] + jnp.sum(g * g * weight, axis=0, keepdims=True)
    both_out[0:1, :half] = low_col[...]
    both_out[0:1, half:] = high_col[...]
    for k, total in enumerate(sums):
        both_out[1:2, k * 128 : (k + 1) * 128] = total


def cols_kernel(n, all_rows, col_prev, *refs):
    parts, (cols_out, by_col_out, total_out) = refs[:n], refs[n:]
    both = tree_sum([p[...] for p in parts])
    total = both[0:1] + small_term * all_rows
    new_cols = decay_rate * col_prev[...] + (1.0 - decay_rate) * total / all_rows
    cols_out[...] = new_cols
    by_col_out[...] = 1.0 / jnp.sqrt(new_cols)
    share = jnp.sum(both[1:2] / new_cols, axis=1, keepdims=True)
    total_out[...] = jnp.broadcast_to(share, total_out.shape)


def factors(elements, parts, by_row, by_col):
    total = tree_sum([part[0:1, 0:1] for part in parts])
    clip = jnp.maximum(1.0, jnp.sqrt(total / elements))
    return by_row[...] / clip, by_col[...]


def fresh_kernel(n, n_pieces, elements, *refs):
    pieces, refs = refs[:n_pieces], refs[n_pieces:]
    (weight, row_factor, col_factor), refs = refs[:3], refs[3:]
    parts, outs = refs[:n], refs[n:]
    by_row, by_col = factors(elements, parts, row_factor, col_factor)
    n_chunks, chunk = by_row.shape
    split = outs[0].shape[0]
    for j in range(n_chunks):
        column = as_column(by_row[j : j + 1])
        first, last = j * chunk, (j + 1) * chunk
        for grads, there in tiles_of(pieces, first, last):
            update = grads * column * by_col[:, there]
            fresh = (weight[first:last, there] - learn_rate * update).astype(jnp.bfloat16)
            if first < split:
                outs[0][first : min(last, split), there] = fresh[: min(last, split) - first]
            if last > split:
                cut = max(first, split)
                outs[1][cut - split : last - split, there] = fresh[cut - first :]


def update_kernel(n, n_pieces, elements, *refs):
    pieces, refs = refs[:n_pieces], refs[n_pieces:]
    (row_factor, col_factor), refs = refs[:2], refs[2:]
    parts, out = refs[:n], refs[n]
    by_row, by_col = factors(elements, parts, row_factor, col_factor)
    n_chunks, chunk = by_row.shape
    for j in range(n_chunks):
        column = as_column(by_row[j : j + 1])
        first, last = j * chunk, (j + 1) * chunk
        for grads, there in tiles_of(pieces, first, last):
            out[first:last, there] = grads * column * by_col[:, there]


def place_kernel(rows_of, *refs):
    pieces, out, sems = refs[: len(rows_of)], refs[-2], refs[-1]
    copies = []
    for k, piece in enumerate(pieces):
        at = pl.ds(pl.multiple_of(rows_of[k](), 16), piece.shape[0])
        copies.append(pltpu.make_async_copy(piece, out.at[at], sems.at[k]))
    for copy in copies:
        copy.start()
    for copy in copies:
        copy.wait()


FAR = pl.BlockSpec(memory_space=pltpu.HBM)
ANYWHERE = pl.BlockSpec(memory_space=pl.ANY)
NEAR = pl.BlockSpec(memory_space=pltpu.VMEM)


def call(kernel, out_shape, *args, flops=0, specs=None, moved=None, **more):
    outs = out_shape if isinstance(out_shape, (tuple, list)) else [out_shape]
    if moved is None:
        moved = sum(x.size * x.dtype.itemsize for x in [*args, *outs])
    return pl.pallas_call(
        kernel,
        out_shape=out_shape,
        in_specs=specs or [NEAR] * len(args),
        compiler_params=pltpu.CompilerParams(vmem_limit_bytes=VMEM_LIMIT),
        cost_estimate=pl.CostEstimate(flops=flops, bytes_accessed=moved, transcendentals=0),
        **more,
    )(*args)


def shape_of(*dims, dtype=jnp.float32):
    return jax.ShapeDtypeStruct(dims, dtype)


def fetch(hidden, grad_out, starts_of, rows):
    if rows % 128 or not starts_of:
        return cut(hidden, starts_of, rows), grad_out
    far = lambda x: pltpu.with_memory_space_constraint(x, pltpu.HBM)
    blocks = [shape_of(hidden.shape[0], rows, dtype=hidden.dtype)] * len(starts_of)
    *blocks, grad_held = call(
        functools.partial(fetch_kernel, starts_of),
        blocks + [shape_of(*grad_out.shape, dtype=grad_out.dtype)],
        far(hidden),
        far(grad_out),
        specs=[FAR, FAR],
        moved=4 * (len(starts_of) * hidden.shape[0] * rows + grad_out.size),
        scratch_shapes=[pltpu.SemaphoreType.DMA((len(starts_of) + 1,))],
    )
    return blocks, grad_held


def cut(hidden, starts_of, rows):
    if rows % 128 or not starts_of:
        return [lax.dynamic_slice_in_dim(hidden, f(), rows, axis=1) for f in starts_of]
    shapes = [shape_of(hidden.shape[0], rows, dtype=hidden.dtype)] * len(starts_of)
    moved = 4 * len(starts_of) * hidden.shape[0] * rows
    return call(functools.partial(cut_kernel, starts_of), shapes, hidden, moved=moved)


def product(held, start_of, rows, peers, gs, coded, bases=(), light=False):
    half = gs[0].shape[1] // 2
    shapes = [
        shape_of(rows + TAIL, half, dtype=jnp.bfloat16) if c else shape_of(rows, half) for c in coded
    ]
    placed = start_of is not None and rows % 128 == 0
    hs = list(peers)
    if placed:
        hs = [held] + hs
    elif start_of is not None:
        hs = [lax.dynamic_slice_in_dim(held, start_of(), rows, axis=1)] + hs
    flops = sum(2 * g.size * rows for g in gs)
    moved = sum(x.size * x.dtype.itemsize for x in [*gs, *bases, *shapes])
    if light:
        flops, moved = 0, 1
    return call(
        functools.partial(product_kernel, (placed, len(hs), len(bases)), start_of, coded),
        shapes,
        *hs,
        *gs,
        *bases,
        flops=flops,
        moved=moved,
    )


def relay(base, messages, group):
    shape = shape_of(group[1] - group[0] + TAIL, base.shape[1], dtype=jnp.bfloat16)
    return call(functools.partial(relay_kernel, len(messages), group), shape, base, *messages)


def gather(base, messages):
    if not messages:
        return base
    return call(gather_kernel, shape_of(*base.shape), base, *messages)


def final(base, messages, group, rows_in, cols_in):
    rows, half = base.shape
    chunk = chunk_of(rows)
    shapes = [
        shape_of(group[1] - group[0], half),
        shape_of(rows // chunk, chunk),
        shape_of(1, half),
    ]
    kernel = functools.partial(
        final_kernel, len(messages), group, rows_in is not None, cols_in is not None
    )
    more = [x for x in (rows_in, cols_in) if x is not None]
    return call(kernel, shapes, base, *messages, *more)


def place(pieces, rows_of, out):
    n = len(pieces)
    old = [] if isinstance(out, jax.ShapeDtypeStruct) else [out]
    return call(
        functools.partial(place_kernel, rows_of),
        jax.ShapeDtypeStruct(out.shape, out.dtype),
        *pieces,
        *old,
        specs=[NEAR] * n + [ANYWHERE] * len(old),
        moved=sum(4 * p.size for p in pieces),
        out_specs=ANYWHERE,
        scratch_shapes=[pltpu.SemaphoreType.DMA((n,))],
        input_output_aliases={n: 0} if old else {},
    )


def after(x, *others):
    return lax.optimization_barrier((x, others))[0]


def grid_of(seq):
    hi = int(math.isqrt(seq))
    while seq % hi:
        hi -= 1
    return hi, seq // hi


def solution(mesh):
    n_dp, n_seq, n_tensor = (mesh.shape[name] for name in ("dp", "seq", "tensor"))
    n_hi, n_lo = grid_of(n_seq)
    his, los = range(1, n_hi), range(1, n_lo)

    def shift(x, hi=0, lo=0):
        pairs = [
            (a * n_lo + b, (a + hi) % n_hi * n_lo + (b + lo) % n_lo)
            for a in range(n_hi)
            for b in range(n_lo)
        ]
        return lax.ppermute(x, "seq", pairs)

    def turn(x, axis, n, step):
        return lax.ppermute(x, axis, [(a, (a + step) % n) for a in range(n)])

    def exchange(parts, axis, n, step=None):
        step = step or (lambda x, d: turn(x, axis, n, d))
        if axis is not None and n == 4:
            x = sum(parts[1:], parts[0])
            swap = lambda d: lax.ppermute(x, axis, [(a, a ^ d) for a in range(n)])
            return [x] + [swap(d) for d in range(1, n)]
        if axis is not None and n & (n - 1) == 0:
            d = 1
            while d < n:
                x = sum(parts[1:], parts[0])
                parts = [x, lax.ppermute(x, axis, [(a, a ^ d) for a in range(n)])]
                d *= 2
            return parts
        if n == 1:
            return parts
        x = sum(parts[1:], parts[0])
        return [x] + [step(x, d) for d in range(1, n)]

    def per_device(hidden, grad_out, master_weight, row_prev, col_prev):
        rows, cols = master_weight.shape

        part_rows = rows // 2
        all_rows, all_cols = rows * n_dp * n_seq, cols * n_tensor

        def block_of(hi, lo):
            seq = lax.axis_index("seq")
            mine = lax.div(seq, n_lo), lax.rem(seq, n_lo)
            return lax.rem(mine[0] + hi, n_hi) * n_lo + lax.rem(mine[1] + lo, n_lo)

        def start_of(p, hi, lo):
            return lambda: (
                lax.rem(lax.axis_index("dp") + p, n_dp) * n_seq + block_of(hi, lo)
            ) * rows

        def row_of(part, hi, lo):
            return lambda: block_of(n_hi - hi, n_lo - lo) * rows + part * part_rows

        gs = [turn(grad_out, "dp", n_dp, p) for p in range(1, n_dp)]
        far_group = [(hi, lo) for hi in his for lo in los]
        near_group = [(0, lo) for lo in los] + [(hi, 0) for hi in his] + [(0, 0)]
        blocks = {at: [] for at in far_group + near_group}
        for group in (far_group, near_group):
            keys = [(p, at) for at in group for p in range(1, n_dp)]
            starts = [start_of(p, *at) for p, at in keys]
            if group is far_group:
                sent, grad_out = fetch(hidden, grad_out, starts, rows)
            else:
                sent = cut(hidden, starts, rows)
            for (p, at), block in zip(keys, sent):
                blocks[at].append(turn(block, "dp", n_dp, p))
        gs = [grad_out] + gs

        far = [{}, {}]
        for hi, lo in far_group:
            bases = product(hidden, start_of(0, hi, lo), rows, [], gs[:1], (False, False))
            if n_dp > 1:
                coded = product(None, None, rows, blocks[hi, lo], gs[1:], (True, True), bases)
            else:
                coded = [relay(x, [], (0, rows)) for x in bases]
            far[0][hi, lo] = shift(coded[0], lo=lo)
            far[1][hi, lo] = shift(coded[1], hi=hi)

        def whole_product(hi, lo, coded):
            peers = blocks[hi, lo]
            return product(hidden, start_of(0, hi, lo), rows, peers, gs, coded, light=True)

        near, base = [{}, {}], [{}, {}]
        for lo in los:
            first, base[1][lo] = whole_product(0, lo, (True, False))
            near[0][lo] = shift(first, lo=lo)
        for hi in his:
            base[0][hi], second = whole_product(hi, 0, (False, True))
            near[1][hi] = shift(second, hi=hi)
        own = whole_product(0, 0, (False, False))
        groups = groups_of(rows)
        last = [{}, {}]
        for group in groups:
            for hi in his:
                message = relay(base[0][hi], [far[0][hi, lo] for lo in los], group)
                last[0].setdefault(group, []).append(shift(message, hi=hi))
            for lo in los:
                message = relay(base[1][lo], [far[1][hi, lo] for hi in his], group)
                last[1].setdefault(group, []).append(shift(message, lo=lo))
        own = [gather(own[part], list(near[part].values())) for part in (0, 1)]
        grads, row_part, col_part = [], None, [None, None]
        for group in groups:
            for part in (0, 1):
                messages = last[part].get(group, [])
                piece, row_part, col_part[part] = final(
                    own[part], messages, group, row_part, col_part[part]
                )
                grads.append(piece)

        chunks = row_part.shape
        parts = exchange([row_part], "tensor", n_tensor)
        new_rows, by_row, both = call(
            functools.partial(rows_kernel, len(parts), len(grads), all_cols),
            [shape_of(*chunks), shape_of(*chunks), shape_of(2, cols)],
            *grads,
            row_prev.reshape(chunks),
            *col_part,
            *parts,
        )
        parts = exchange([both], "dp", n_dp)
        x = sum(parts[1:], parts[0])
        if n_hi * n_lo <= 4:
            steps = [(hi, lo) for hi in range(n_hi) for lo in range(n_lo) if hi or lo]
            parts = [x] + [shift(x, hi=hi, lo=lo) for hi, lo in steps]
        else:
            parts = exchange([x], None, n_lo, lambda x, d: shift(x, lo=d))
            parts = exchange(parts, None, n_hi, lambda x, d: shift(x, hi=d))
        new_cols, by_col, share = call(
            functools.partial(cols_kernel, len(parts), all_rows),
            [shape_of(1, cols), shape_of(1, cols), shape_of(1, 128)],
            col_prev.reshape(1, cols),
            *parts,
        )
        parts = exchange([share], "tensor", n_tensor)
        elements = all_rows * all_cols

        pair = call(
            functools.partial(fresh_kernel, len(parts), len(grads), elements),
            [shape_of(part_rows, cols, dtype=jnp.bfloat16)] * 2,
            *grads,
            master_weight,
            by_row,
            by_col,
            *parts,
        )
        along_lo, along_hi = {}, {}
        for lo in los:
            along_lo[0, lo] = shift(pair[0], lo=lo)
        for hi in his:
            along_hi[1, hi] = shift(pair[1], hi=hi)
        for lo in los:
            along_lo[1, lo] = shift(pair[1], lo=lo)
        for hi in his:
            along_hi[0, hi] = shift(pair[0], hi=hi)

        onward = []
        for hi in his:
            for lo in los:
                onward.append((shift(along_lo[0, lo], hi=hi), row_of(0, hi, lo)))
                onward.append((shift(along_hi[1, hi], lo=lo), row_of(1, hi, lo)))
        update = call(
            functools.partial(update_kernel, len(parts), len(grads), elements),
            shape_of(rows, cols),
            after(grads[0], *along_lo.values()),
            *grads[1:],
            by_row,
            by_col,
            *parts,
        )

        whole = jax.ShapeDtypeStruct((rows * n_seq, cols), jnp.bfloat16)
        new_weight = place(pair, [row_of(part, 0, 0) for part in (0, 1)], whole)
        pieces = [(x, row_of(part, 0, lo)) for (part, lo), x in along_lo.items()]
        pieces += [(x, row_of(part, hi, 0)) for (part, hi), x in along_hi.items()]
        for group in [pieces, onward]:
            if group:
                new_weight = place([x for x, _ in group], [f for _, f in group], new_weight)
        return (new_weight, update, new_rows.reshape(rows), new_cols.reshape(cols))

    return jax.shard_map(
        per_device,
        mesh=mesh,
        in_specs=(
            P(("dp", "seq"), None),
            P(("dp", "seq"), "tensor"),
            P(("dp", "seq"), "tensor"),
            P(("dp", "seq")),
            P("tensor"),
        ),
        out_specs=(P("dp", "tensor"), P(("dp", "seq"), "tensor"), P(("dp", "seq")), P("tensor")),
        check_vma=False,
    )
```

```python
import functools
import math

import jax
import jax.numpy as jnp
from jax import lax
from jax.experimental import pallas as pl
from jax.experimental.pallas import tpu as pltpu
from jax.sharding import PartitionSpec as P

decay_rate = 0.8
learn_rate = 0.05
small_term = 1e-06

POWER = 11
TOP = 2.0 ** (125.0 / POWER)
TAIL = 16
VMEM_LIMIT = 16 * 2**20


def chunk_of(rows):
    return 128 if rows % 128 == 0 else rows


def groups_of(rows):
    n = rows // chunk_of(rows)
    cuts = sorted({0, n - 1, n})
    return [(a * chunk_of(rows), b * chunk_of(rows)) for a, b in zip(cuts, cuts[1:])]


def encode(x):
    top = jnp.max(jnp.abs(x), axis=0, keepdims=True)
    scale = jnp.maximum(top * 1.004, 1e-30).astype(jnp.bfloat16).astype(jnp.float32)
    u = x * (TOP / scale)
    u2 = u * u
    u4 = u2 * u2
    return (u4 * u4 * u2 * u).astype(jnp.bfloat16), scale


def decode(code, scale):
    code = code.astype(jnp.float32)
    size = jnp.abs(code)
    u = jnp.exp(jnp.log(jnp.maximum(size, 1e-37)) * (1.0 / POWER)) * (scale * (1.0 / TOP))
    return jnp.where(size > 1e-37, jnp.where(code > 0, u, -u), 0.0)


def write_scales(ref, scales):
    rows, cols = ref.shape
    at = lax.broadcasted_iota(jnp.int32, (TAIL, cols), 0)
    tail = jnp.zeros((TAIL, cols), jnp.float32)
    for j, scale in enumerate(scales):
        tail = jnp.where(at == j, scale, tail)
    ref[rows - TAIL :] = tail.astype(jnp.bfloat16)


def read_scales(ref):
    return ref[ref.shape[0] - TAIL :].astype(jnp.float32)


def product_kernel(layout, start_of, coded, *refs):
    placed, n_hs, n_base = layout
    refs = list(refs)
    take = lambda k: [refs.pop(0) for _ in range(k)]
    hs, gs, bases, outs = take(n_hs), take(n_hs), take(n_base), refs
    cols = gs[0].shape[1]
    rows = outs[0].shape[0] - (TAIL if coded[0] else 0)
    half, chunk = cols // 2, chunk_of(rows)
    first = [start_of() if k == 0 and placed else 0 for k in range(n_hs)]
    scales = [[], []]
    for j in range(rows // chunk):
        at = slice(j * chunk, (j + 1) * chunk)
        total = None
        for k, (h, g) in enumerate(zip(hs, gs)):
            if k == 0 and placed:
                block = h[:, pl.ds(pl.multiple_of(first[k] + j * chunk, chunk), chunk)]
            else:
                block = h[:, at]
            term = lax.dot_general(
                block, g[...], (((0,), (0,)), ((), ())), preferred_element_type=jnp.float32
            )
            total = term if total is None else total + term
        for part in (0, 1):
            x = total[:, part * half : (part + 1) * half]
            if bases:
                x = x + bases[part][at]
            if coded[part]:
                outs[part][at], scale = encode(x)
                scales[part].append(scale)
            else:
                outs[part][at] = x
    for part in (0, 1):
        if coded[part]:
            write_scales(outs[part], scales[part])


def fetch_kernel(starts_of, hidden, grad_out, *refs):
    outs, grad_held, sems = refs[:-2], refs[-2], refs[-1]
    copies = []
    for k, (start_of, out) in enumerate(zip(starts_of, outs)):
        at = pl.ds(pl.multiple_of(start_of(), 128), out.shape[1])
        copies.append(pltpu.make_async_copy(hidden.at[:, at], out, sems.at[k]))
        copies[k].start()
    copies.append(pltpu.make_async_copy(grad_out, grad_held, sems.at[len(outs)]))
    copies[-1].start()
    for copy in copies:
        copy.wait()


def cut_kernel(starts_of, hidden, *outs):
    for start_of, out in zip(starts_of, outs):
        out[...] = hidden[:, pl.ds(pl.multiple_of(start_of(), 128), out.shape[1])]


def added_up(base, messages, group, begin):
    chunk = chunk_of(base.shape[0])
    tails = [read_scales(m) for m in messages]
    for row in range(*group, chunk):
        total = base[row : row + chunk]
        j = (row - begin) // chunk
        for m, tail in zip(messages, tails):
            total = total + decode(m[row - begin : row - begin + chunk], tail[j : j + 1])
        yield slice(row, row + chunk), total


def relay_kernel(n, group, base, *refs):
    messages, out = refs[:n], refs[n]
    scales = []
    for at, total in added_up(base, messages, group, 0):
        out[at.start - group[0] : at.stop - group[0]], scale = encode(total)
        scales.append(scale)
    write_scales(out, scales)


def gather_kernel(base, *refs):
    messages, out = refs[:-1], refs[-1]
    for at, total in added_up(base, messages, (0, base.shape[0]), 0):
        out[at] = total


def final_kernel(n, group, has_rows, has_cols, base, *refs):
    refs = list(refs)
    messages = [refs.pop(0) for _ in range(n)]
    rows_in = refs.pop(0)[...] if has_rows else None
    cols_in = refs.pop(0)[...] if has_cols else 0.0
    out, row_out, col_out = refs
    chunk, half = chunk_of(base.shape[0]), base.shape[1]
    row_out[...] = rows_in if has_rows else jnp.zeros(row_out.shape, jnp.float32)
    col_sum = jnp.zeros((1, half), jnp.float32) + cols_in
    for at, total in added_up(base, messages, group, group[0]):
        out[at.start - group[0] : at.stop - group[0]] = total
        squares = total * total
        col_sum = col_sum + jnp.sum(squares, axis=0, keepdims=True)
        row_sum = jnp.zeros((chunk, 128), jnp.float32)
        for k in range(half // 128):
            row_sum = row_sum + squares[:, k * 128 : (k + 1) * 128]
        row_sum = jnp.sum(row_sum.T, axis=0, keepdims=True)
        j = at.start // chunk
        row_out[j : j + 1] = row_sum + (rows_in[j : j + 1] if has_rows else 0.0)
    col_out[...] = col_sum


def tiles_of(pieces, first, last):
    half, begin = pieces[0].shape[1], 0
    for low, high in zip(pieces[::2], pieces[1::2]):
        end = begin + low.shape[0]
        if begin <= first < end:
            for part, ref in enumerate((low, high)):
                for k in range(0, half, 128):
                    tile = ref[first - begin : last - begin, k : k + 128]
                    yield tile, slice(part * half + k, part * half + k + 128)
        begin = end


def as_column(row):
    return jnp.broadcast_to(row, (128, row.shape[1])).T


def tree_sum(terms):
    while len(terms) > 1:
        pairs = [sum(terms[k + 1 : k + 2], terms[k]) for k in range(0, len(terms), 2)]
        terms = pairs
    return terms[0]


def rows_kernel(n, n_pieces, all_cols, *refs):
    pieces, refs = refs[:n_pieces], refs[n_pieces:]
    (row_prev, low_col, high_col), refs = refs[:3], refs[3:]
    parts, (rows_out, by_row_out, both_out) = refs[:n], refs[n:]
    total = tree_sum([p[...] for p in parts])
    total = total + small_term * all_cols
    new_rows = decay_rate * row_prev[...] + (1.0 - decay_rate) * total / all_cols
    rows_out[...] = new_rows
    by_row_out[...] = 1.0 / jnp.sqrt(new_rows)
    inverse = 1.0 / new_rows
    n_chunks, chunk = new_rows.shape
    half = low_col.shape[1]
    sums = [jnp.zeros((1, 128), jnp.float32)] * (2 * half // 128)
    for j in range(n_chunks):
        weight = as_column(inverse[j : j + 1])
        for k, (g, _) in enumerate(tiles_of(pieces, j * chunk, (j + 1) * chunk)):
            sums[k] = sums[k] + jnp.sum(g * g * weight, axis=0, keepdims=True)
    both_out[0:1, :half] = low_col[...]
    both_out[0:1, half:] = high_col[...]
    for k, total in enumerate(sums):
        both_out[1:2, k * 128 : (k + 1) * 128] = total


def cols_kernel(n, all_rows, col_prev, *refs):
    parts, (cols_out, by_col_out, total_out) = refs[:n], refs[n:]
    both = tree_sum([p[...] for p in parts])
    total = both[0:1] + small_term * all_rows
    new_cols = decay_rate * col_prev[...] + (1.0 - decay_rate) * total / all_rows
    cols_out[...] = new_cols
    by_col_out[...] = 1.0 / jnp.sqrt(new_cols)
    share = jnp.sum(both[1:2] / new_cols, axis=1, keepdims=True)
    total_out[...] = jnp.broadcast_to(share, total_out.shape)


def factors(elements, parts, by_row, by_col):
    total = tree_sum([part[0:1, 0:1] for part in parts])
    clip = jnp.maximum(1.0, jnp.sqrt(total / elements))
    return by_row[...] / clip, by_col[...]


def fresh_kernel(n, n_pieces, elements, *refs):
    pieces, refs = refs[:n_pieces], refs[n_pieces:]
    (weight, row_factor, col_factor), refs = refs[:3], refs[3:]
    parts, outs = refs[:n], refs[n:]
    by_row, by_col = factors(elements, parts, row_factor, col_factor)
    n_chunks, chunk = by_row.shape
    split = outs[0].shape[0]
    for j in range(n_chunks):
        column = as_column(by_row[j : j + 1])
        first, last = j * chunk, (j + 1) * chunk
        for grads, there in tiles_of(pieces, first, last):
            update = grads * column * by_col[:, there]
            fresh = (weight[first:last, there] - learn_rate * update).astype(jnp.bfloat16)
            if first < split:
                outs[0][first : min(last, split), there] = fresh[: min(last, split) - first]
            if last > split:
                cut = max(first, split)
                outs[1][cut - split : last - split, there] = fresh[cut - first :]


def update_kernel(n, n_pieces, elements, *refs):
    pieces, refs = refs[:n_pieces], refs[n_pieces:]
    (row_factor, col_factor), refs = refs[:2], refs[2:]
    parts, out = refs[:n], refs[n]
    by_row, by_col = factors(elements, parts, row_factor, col_factor)
    n_chunks, chunk = by_row.shape
    for j in range(n_chunks):
        column = as_column(by_row[j : j + 1])
        first, last = j * chunk, (j + 1) * chunk
        for grads, there in tiles_of(pieces, first, last):
            out[first:last, there] = grads * column * by_col[:, there]


def place_kernel(rows_of, *refs):
    pieces, out, sems = refs[: len(rows_of)], refs[-2], refs[-1]
    copies = []
    for k, piece in enumerate(pieces):
        at = pl.ds(pl.multiple_of(rows_of[k](), 16), piece.shape[0])
        copies.append(pltpu.make_async_copy(piece, out.at[at], sems.at[k]))
    for copy in copies:
        copy.start()
    for copy in copies:
        copy.wait()


FAR = pl.BlockSpec(memory_space=pltpu.HBM)
ANYWHERE = pl.BlockSpec(memory_space=pl.ANY)
NEAR = pl.BlockSpec(memory_space=pltpu.VMEM)


def call(kernel, out_shape, *args, flops=0, specs=None, moved=None, **more):
    outs = out_shape if isinstance(out_shape, (tuple, list)) else [out_shape]
    if moved is None:
        moved = sum(x.size * x.dtype.itemsize for x in [*args, *outs])
    return pl.pallas_call(
        kernel,
        out_shape=out_shape,
        in_specs=specs or [NEAR] * len(args),
        compiler_params=pltpu.CompilerParams(vmem_limit_bytes=VMEM_LIMIT),
        cost_estimate=pl.CostEstimate(flops=flops, bytes_accessed=moved, transcendentals=0),
        **more,
    )(*args)


def shape_of(*dims, dtype=jnp.float32):
    return jax.ShapeDtypeStruct(dims, dtype)


def fetch(hidden, grad_out, starts_of, rows):
    if rows % 128 or not starts_of:
        return cut(hidden, starts_of, rows), grad_out
    far = lambda x: pltpu.with_memory_space_constraint(x, pltpu.HBM)
    blocks = [shape_of(hidden.shape[0], rows, dtype=hidden.dtype)] * len(starts_of)
    *blocks, grad_held = call(
        functools.partial(fetch_kernel, starts_of),
        blocks + [shape_of(*grad_out.shape, dtype=grad_out.dtype)],
        far(hidden),
        far(grad_out),
        specs=[FAR, FAR],
        moved=4 * (len(starts_of) * hidden.shape[0] * rows + grad_out.size),
        scratch_shapes=[pltpu.SemaphoreType.DMA((len(starts_of) + 1,))],
    )
    return blocks, grad_held


def cut(hidden, starts_of, rows):
    if rows % 128 or not starts_of:
        return [lax.dynamic_slice_in_dim(hidden, f(), rows, axis=1) for f in starts_of]
    shapes = [shape_of(hidden.shape[0], rows, dtype=hidden.dtype)] * len(starts_of)
    moved = 4 * len(starts_of) * hidden.shape[0] * rows
    return call(functools.partial(cut_kernel, starts_of), shapes, hidden, moved=moved)


def product(held, start_of, rows, peers, gs, coded, bases=(), light=False):
    half = gs[0].shape[1] // 2
    shapes = [
        shape_of(rows + TAIL, half, dtype=jnp.bfloat16) if c else shape_of(rows, half) for c in coded
    ]
    placed = start_of is not None and rows % 128 == 0
    hs = list(peers)
    if placed:
        hs = [held] + hs
    elif start_of is not None:
        hs = [lax.dynamic_slice_in_dim(held, start_of(), rows, axis=1)] + hs
    flops = sum(2 * g.size * rows for g in gs)
    moved = sum(x.size * x.dtype.itemsize for x in [*gs, *bases, *shapes])
    if light:
        flops, moved = 0, 1
    return call(
        functools.partial(product_kernel, (placed, len(hs), len(bases)), start_of, coded),
        shapes,
        *hs,
        *gs,
        *bases,
        flops=flops,
        moved=moved,
    )


def relay(base, messages, group):
    shape = shape_of(group[1] - group[0] + TAIL, base.shape[1], dtype=jnp.bfloat16)
    return call(functools.partial(relay_kernel, len(messages), group), shape, base, *messages)


def gather(base, messages):
    if not messages:
        return base
    return call(gather_kernel, shape_of(*base.shape), base, *messages)


def final(base, messages, group, rows_in, cols_in):
    rows, half = base.shape
    chunk = chunk_of(rows)
    shapes = [
        shape_of(group[1] - group[0], half),
        shape_of(rows // chunk, chunk),
        shape_of(1, half),
    ]
    kernel = functools.partial(
        final_kernel, len(messages), group, rows_in is not None, cols_in is not None
    )
    more = [x for x in (rows_in, cols_in) if x is not None]
    return call(kernel, shapes, base, *messages, *more)


def place(pieces, rows_of, out):
    n = len(pieces)
    old = [] if isinstance(out, jax.ShapeDtypeStruct) else [out]
    return call(
        functools.partial(place_kernel, rows_of),
        jax.ShapeDtypeStruct(out.shape, out.dtype),
        *pieces,
        *old,
        specs=[NEAR] * n + [ANYWHERE] * len(old),
        moved=sum(4 * p.size for p in pieces),
        out_specs=ANYWHERE,
        scratch_shapes=[pltpu.SemaphoreType.DMA((n,))],
        input_output_aliases={n: 0} if old else {},
    )


def after(x, *others):
    return lax.optimization_barrier((x, others))[0]


def grid_of(seq):
    hi = int(math.isqrt(seq))
    while seq % hi:
        hi -= 1
    return hi, seq // hi


def solution(mesh):
    n_dp, n_seq, n_tensor = (mesh.shape[name] for name in ("dp", "seq", "tensor"))
    n_hi, n_lo = grid_of(n_seq)
    his, los = range(1, n_hi), range(1, n_lo)

    def shift(x, hi=0, lo=0):
        pairs = [
            (a * n_lo + b, (a + hi) % n_hi * n_lo + (b + lo) % n_lo)
            for a in range(n_hi)
            for b in range(n_lo)
        ]
        return lax.ppermute(x, "seq", pairs)

    def turn(x, axis, n, step):
        return lax.ppermute(x, axis, [(a, (a + step) % n) for a in range(n)])

    def exchange(parts, axis, n, step=None):
        step = step or (lambda x, d: turn(x, axis, n, d))
        if axis is not None and n == 4:
            x = sum(parts[1:], parts[0])
            swap = lambda d: lax.ppermute(x, axis, [(a, a ^ d) for a in range(n)])
            return [x] + [swap(d) for d in reversed(range(1, n))]
        if axis is not None and n & (n - 1) == 0:
            d = 1
            while d < n:
                x = sum(parts[1:], parts[0])
                parts = [x, lax.ppermute(x, axis, [(a, a ^ d) for a in range(n)])]
                d *= 2
            return parts
        if n == 1:
            return parts
        x = sum(parts[1:], parts[0])
        return [x] + [step(x, d) for d in range(1, n)]

    def per_device(hidden, grad_out, master_weight, row_prev, col_prev):
        rows, cols = master_weight.shape

        part_rows = rows // 2
        all_rows, all_cols = rows * n_dp * n_seq, cols * n_tensor

        def block_of(hi, lo):
            seq = lax.axis_index("seq")
            mine = lax.div(seq, n_lo), lax.rem(seq, n_lo)
            return lax.rem(mine[0] + hi, n_hi) * n_lo + lax.rem(mine[1] + lo, n_lo)

        def start_of(p, hi, lo):
            return lambda: (
                lax.rem(lax.axis_index("dp") + p, n_dp) * n_seq + block_of(hi, lo)
            ) * rows

        def row_of(part, hi, lo):
            return lambda: block_of(n_hi - hi, n_lo - lo) * rows + part * part_rows

        gs = [turn(grad_out, "dp", n_dp, p) for p in range(1, n_dp)]
        far_group = [(hi, lo) for hi in his for lo in los]
        near_group = [(0, lo) for lo in los] + [(hi, 0) for hi in his] + [(0, 0)]
        blocks = {at: [] for at in far_group + near_group}
        for group in (far_group, near_group):
            keys = [(p, at) for at in group for p in range(1, n_dp)]
            starts = [start_of(p, *at) for p, at in keys]
            if group is far_group:
                sent, grad_out = fetch(hidden, grad_out, starts, rows)
            else:
                sent = cut(hidden, starts, rows)
            for (p, at), block in zip(keys, sent):
                blocks[at].append(turn(block, "dp", n_dp, p))
        gs = [grad_out] + gs

        far = [{}, {}]
        for hi, lo in far_group:
            bases = product(hidden, start_of(0, hi, lo), rows, [], gs[:1], (False, False))
            if n_dp > 1:
                coded = product(None, None, rows, blocks[hi, lo], gs[1:], (True, True), bases)
            else:
                coded = [relay(x, [], (0, rows)) for x in bases]
            far[0][hi, lo] = shift(coded[0], lo=lo)
            far[1][hi, lo] = shift(coded[1], hi=hi)

        def whole_product(hi, lo, coded):
            peers = blocks[hi, lo]
            return product(hidden, start_of(0, hi, lo), rows, peers, gs, coded, light=True)

        near, base = [{}, {}], [{}, {}]
        for lo in los:
            first, base[1][lo] = whole_product(0, lo, (True, False))
            near[0][lo] = shift(first, lo=lo)
        for hi in his:
            base[0][hi], second = whole_product(hi, 0, (False, True))
            near[1][hi] = shift(second, hi=hi)
        own = whole_product(0, 0, (False, False))
        groups = groups_of(rows)
        last = [{}, {}]
        for group in groups:
            for hi in his:
                message = relay(base[0][hi], [far[0][hi, lo] for lo in los], group)
                last[0].setdefault(group, []).append(shift(message, hi=hi))
            for lo in los:
                message = relay(base[1][lo], [far[1][hi, lo] for hi in his], group)
                last[1].setdefault(group, []).append(shift(message, lo=lo))
        own = [gather(own[part], list(near[part].values())) for part in (0, 1)]
        grads, row_part, col_part = [], None, [None, None]
        for group in groups:
            for part in (0, 1):
                messages = last[part].get(group, [])
                piece, row_part, col_part[part] = final(
                    own[part], messages, group, row_part, col_part[part]
                )
                grads.append(piece)

        chunks = row_part.shape
        parts = exchange([row_part], "tensor", n_tensor)
        new_rows, by_row, both = call(
            functools.partial(rows_kernel, len(parts), len(grads), all_cols),
            [shape_of(*chunks), shape_of(*chunks), shape_of(2, cols)],
            *grads,
            row_prev.reshape(chunks),
            *col_part,
            *parts,
        )
        parts = exchange([both], "dp", n_dp)
        x = sum(parts[1:], parts[0])
        if n_hi * n_lo <= 4:
            steps = [(hi, lo) for hi in range(n_hi) for lo in range(n_lo) if hi or lo]
            parts = [x] + [shift(x, hi=hi, lo=lo) for hi, lo in reversed(steps)]
        else:
            parts = exchange([x], None, n_lo, lambda x, d: shift(x, lo=d))
            parts = exchange(parts, None, n_hi, lambda x, d: shift(x, hi=d))
        new_cols, by_col, share = call(
            functools.partial(cols_kernel, len(parts), all_rows),
            [shape_of(1, cols), shape_of(1, cols), shape_of(1, 128)],
            col_prev.reshape(1, cols),
            *parts,
        )
        parts = exchange([share], "tensor", n_tensor)
        elements = all_rows * all_cols

        pair = call(
            functools.partial(fresh_kernel, len(parts), len(grads), elements),
            [shape_of(part_rows, cols, dtype=jnp.bfloat16)] * 2,
            *grads,
            master_weight,
            by_row,
            by_col,
            *parts,
        )
        along_lo, along_hi = {}, {}
        for lo in los:
            along_lo[0, lo] = shift(pair[0], lo=lo)
        for hi in his:
            along_hi[1, hi] = shift(pair[1], hi=hi)
        for lo in los:
            along_lo[1, lo] = shift(pair[1], lo=lo)
        for hi in his:
            along_hi[0, hi] = shift(pair[0], hi=hi)

        onward = []
        for hi in his:
            for lo in los:
                onward.append((shift(along_lo[0, lo], hi=hi), row_of(0, hi, lo)))
                onward.append((shift(along_hi[1, hi], lo=lo), row_of(1, hi, lo)))
        update = call(
            functools.partial(update_kernel, len(parts), len(grads), elements),
            shape_of(rows, cols),
            after(grads[0], *along_lo.values()),
            *grads[1:],
            by_row,
            by_col,
            *parts,
        )

        whole = jax.ShapeDtypeStruct((rows * n_seq, cols), jnp.bfloat16)
        new_weight = place(pair, [row_of(part, 0, 0) for part in (0, 1)], whole)
        pieces = [(x, row_of(part, 0, lo)) for (part, lo), x in along_lo.items()]
        pieces += [(x, row_of(part, hi, 0)) for (part, hi), x in along_hi.items()]
        for group in [pieces, onward]:
            if group:
                new_weight = place([x for x, _ in group], [f for _, f in group], new_weight)
        return (new_weight, update, new_rows.reshape(rows), new_cols.reshape(cols))

    return jax.shard_map(
        per_device,
        mesh=mesh,
        in_specs=(
            P(("dp", "seq"), None),
            P(("dp", "seq"), "tensor"),
            P(("dp", "seq"), "tensor"),
            P(("dp", "seq")),
            P("tensor"),
        ),
        out_specs=(P("dp", "tensor"), P(("dp", "seq"), "tensor"), P(("dp", "seq")), P("tensor")),
        check_vma=False,
    )
```
